32 devices in a mesh: dp: 4 (over y, core), pipe: 4 (over z), ctx: 2 (over x).
Axes of the slice: x: 2, y: 2, z: 4, core: 2. Of those that a mesh axis runs over, the one named last changes fastest.
Arguments:
- acts: bfloat16 [4, 4, 4, 544, 8192], P('dp', 'pipe', None, 'ctx'), may hold values from -0.25 to 0.25
- key_grads: bfloat16 [4, 4, 4, 544, 512], P('dp', 'pipe', None, 'ctx'), may hold values from -6 to 6
- weights: bfloat16 [4, 8192, 512], P('pipe', 'ctx'), may hold values from -0.25 to 0.25
- b_slot: int32 [4], P('pipe'), may hold values from 0 to 3
- cycle: int32 [8], replicated, may hold values from 0 to 7, each once
Outputs:
- passed_grad: bfloat16 [4, 4, 544, 8192], P('dp', 'pipe', 'ctx')
- weight_grad: float32 [4, 8192, 512], P('pipe', 'ctx')
The draws below stay inside these ranges and needn't reach their ends.
Inputs may be any that keep to these rules, and one draw needn't show every extreme that they name: `cycle`: each value once.
All inputs are finite; a program needn't handle non-finite values.
Results may differ from the reference program's by a relative error of at most 0.001.
Values may be sent and summed in bfloat16 or wider, within the bound.
No kernel may reach another device: no remote copies, remote signals or barrier semaphores. Data moves between devices by JAX's collectives and lax.ppermute only.
A program may use at most 192 MiB of HBM per device.

```python
import jax
import jax.numpy as jnp
from jax import lax

D = 8192
KW = 512
MB = 4
ROWS = 272
SEQ_ROWS = 544
PIECES = 8
N_DP = 4
N_PIPE = 4
N_CTX = 2


def set_ends(entries, key, low, high):
    shape = entries.shape
    place = [jax.random.randint(jax.random.fold_in(key, axis), (), 0, shape[axis]) for axis in range(len(shape))]
    entries = entries.at[tuple(place)].set(low)
    longest = shape.index(max(shape))
    place[longest] = (place[longest] + 1) % shape[longest]
    return entries.at[tuple(place)].set(high)


def spiked(drawn, rng, source, target, blocks, factor):
    def block_of(dim):
        return (jnp.arange(drawn.shape[dim]) // (drawn.shape[dim] // blocks)).reshape((-1,) + (1,) * (drawn.ndim - 1 - dim))

    one_side = jax.random.permutation(rng, blocks)[block_of(target)]
    other_side = (block_of(target) + blocks // 2) % blocks
    return jnp.where((block_of(source) == one_side) | (block_of(source) == other_side), factor * drawn, drawn)


def levels(stream_key, extent, split, low, largest):
    def one(dim, parts):
        steps = jax.random.uniform(jax.random.fold_in(jax.random.fold_in(stream_key, 6), dim), (parts,), jnp.float32, low / len(split), largest / len(split))
        return jnp.repeat(jnp.exp(steps), extent[dim] // parts).reshape((-1,) + (1,) * (len(extent) - dim - 1))

    factor_of = one(*split[0])
    for cut in split[1:]:
        factor_of = factor_of * one(*cut)
    return factor_of


def noise(key, dims, spread, bound, split=(), kind=jnp.bfloat16):
    array = spread * jax.random.normal(key, dims, jnp.float32)
    if split:
        array = array * levels(key, dims, split, -0.22, 0.18)
    return jnp.clip(array, -bound, bound).astype(kind)


def gaussian_with(key, dims, scale, limit, split, heavy, kind=jnp.bfloat16):
    array = scale * jax.random.normal(key, dims, jnp.float32)
    if split:
        array = array * levels(key, dims, split, -0.22, 0.18)
    return jnp.clip(spiked(array, jax.random.fold_in(key, 3), *heavy), -limit, limit).astype(kind)


def setup_inputs(seed: int = 0) -> dict:
    keys = jax.random.split(jax.random.key(seed), 6)
    acts = gaussian_with(keys[0], (N_DP, N_PIPE, MB, SEQ_ROWS, D), (1.0 / (N_DP * (MB - 1) * ROWS * N_CTX) ** 0.5), 0.25, ((0, 4), (1, 4), (3, 2)), (3, 4, 2, 2.0))
    key_grads = noise(keys[1], (N_DP, N_PIPE, MB, SEQ_ROWS, KW), 1.0, 6.0, ((0, 4), (1, 4), (3, 2)))
    weights = noise(keys[2], (N_PIPE, D, KW), KW ** -0.5, 0.25, ((0, 4), (1, 2)))
    b_slot = set_ends(jax.random.randint(keys[3], (N_PIPE,), 0, MB), jax.random.fold_in(keys[3], 1), 0, MB - 1).astype(jnp.int32)
    cycle = jax.random.permutation(keys[4], PIECES).astype(jnp.int32)
    return dict(acts=acts, key_grads=key_grads, weights=weights, b_slot=b_slot, cycle=cycle)


def reference(acts, key_grads, weights, b_slot, cycle):
    section_list = []
    grad_list = []
    micro = jnp.arange(MB, dtype=jnp.int32)
    for section in range(N_PIPE):
        slot_index = b_slot[section]
        current = lax.dynamic_index_in_dim(key_grads[:, section], slot_index, 1, keepdims=False).reshape(-1, KW)
        section_grad = lax.dot_general(current, weights[section], (((1,), (1,)), ((), ())), preferred_element_type=jnp.float32).astype(jnp.bfloat16)
        section_list.append(section_grad.reshape(N_DP, SEQ_ROWS, D))
        keeper = (micro != slot_index)[None, :, None, None]
        masked = jnp.where(keeper, key_grads[:, section], jnp.zeros((), key_grads.dtype)).reshape(-1, KW)
        full_grad = lax.dot_general(acts[:, section].reshape(-1, D), masked, (((0,), (0,)), ((), ())), preferred_element_type=jnp.float32)
        grad_list.append(full_grad.reshape(PIECES, D // PIECES, KW)[cycle].reshape(D, KW))
    shifted = section_list[1:] + [jnp.zeros_like(section_list[0])]
    return jnp.stack(shifted, axis=1), jnp.stack(grad_list, axis=0)
```

```python
import functools

import jax
import jax.numpy as jnp
from jax import lax
from jax.experimental import pallas as pl
from jax.experimental.pallas import tpu as pltpu
from jax.sharding import PartitionSpec as P

LANES = 128
TAIL = 16
INNER = 2
TOP = 32767.0
VMEM_LIMIT = 48 << 20


def params():
    return pltpu.CompilerParams(vmem_limit_bytes=VMEM_LIMIT)


def code_shape(rows, width):
    return jax.ShapeDtypeStruct((width // LANES * rows + TAIL, LANES), jnp.int16)


def scale_of(code_ref, count):
    exponent = code_ref[count : count + TAIL, :].astype(jnp.int32)[0:1, :].astype(jnp.float32)
    return jnp.exp2(exponent) * (1.0 / (TOP * TOP))


def decoded(code_ref, start, rows, scale):
    level = code_ref[pl.ds(start, rows), :].astype(jnp.int32).astype(jnp.float32)
    return level * jnp.abs(level) * scale


def combine_kernel(*refs, n_sums, n_codes, rows, width):
    sums = refs[:n_sums]
    codes = refs[n_sums : n_sums + n_codes]
    out_ref = refs[n_sums + n_codes]
    total_ref = refs[n_sums + n_codes + 1]
    slabs = width // LANES
    step = min(rows, 128)
    scales = [scale_of(c, slabs * rows) for c in codes]

    def add(i, largest):
        r = pl.multiple_of(i * step, step)
        for j in range(slabs):
            value = sums[0][0, pl.ds(r, step), j * LANES : (j + 1) * LANES]
            for s in sums[1:]:
                value = value + s[0, pl.ds(r, step), j * LANES : (j + 1) * LANES]
            for c, scale in zip(codes, scales):
                value = value + decoded(c, pl.multiple_of(j * rows + r, step), step, scale)
            total_ref[pl.ds(r, step), j * LANES : (j + 1) * LANES] = value
            folded = jnp.abs(value).reshape(step // 8, 8, LANES)
            largest = jnp.maximum(largest, jnp.max(folded, axis=0))
        return largest

    largest = lax.fori_loop(0, rows // step, add, jnp.zeros((8, LANES), jnp.float32))
    largest = jnp.max(jnp.max(largest, axis=0, keepdims=True), axis=1, keepdims=True)
    exponent = jnp.floor(jnp.log2(jnp.maximum(largest, 1e-30))) + 2.0
    exponent = jnp.broadcast_to(exponent, (8, LANES))
    shrink = jnp.exp2(-exponent)[0:1, :]

    def encode(i, carry):
        r = pl.multiple_of(i * step, step)
        for j in range(slabs):
            value = total_ref[pl.ds(r, step), j * LANES : (j + 1) * LANES]
            root = jnp.round(jnp.sqrt(jnp.abs(value) * shrink) * TOP)
            level = jnp.where(value < 0.0, -root, root)
            place = pl.ds(pl.multiple_of(j * rows + r, step), step)
            out_ref[place, :] = level.astype(jnp.int32).astype(jnp.int16)
        return carry

    lax.fori_loop(0, rows // step, encode, 0)
    tail = jnp.concatenate([exponent] * (TAIL // 8), axis=0)
    out_ref[slabs * rows : slabs * rows + TAIL, :] = tail.astype(jnp.int32).astype(jnp.int16)


def combine(sums, codes, rows, width):
    shape = code_shape(rows, width)
    in_specs = [
        pl.BlockSpec((1, rows, width), functools.partial(lambda at, i: (at, 0, 0), at)) for _, at in sums
    ] + [pl.BlockSpec(shape.shape, lambda i: (0, 0)) for _ in codes]
    return pl.pallas_call(
        functools.partial(combine_kernel, n_sums=len(sums), n_codes=len(codes), rows=rows, width=width),
        out_shape=shape,
        grid=(1,),
        in_specs=in_specs,
        out_specs=pl.BlockSpec(shape.shape, lambda i: (0, 0)),
        scratch_shapes=[pltpu.VMEM((rows, width), jnp.float32)],
        compiler_params=params(),
        cost_estimate=pl.CostEstimate(
            flops=20 * rows * width,
            bytes_accessed=rows * width * (4 * len(sums) + 2 * len(codes) + 2),
            transcendentals=0,
        ),
    )(*[a for a, _ in sums], *codes)


def token_kernel(order, picks, *refs, count):
    left = jnp.concatenate([r[0] for r in refs[:count]], axis=0)
    right = jnp.concatenate([r[0] for r in refs[count : 2 * count]], axis=0)
    refs[2 * count][0] = lax.dot_general(
        left, right, (((0,), (0,)), ((), ())), preferred_element_type=jnp.float32
    )


def token_products(order, picks, acts, grads, block, rows):
    steps = order.shape[0]
    count = picks.shape[0]
    tokens = acts.shape[1]
    width = grads.shape[2]
    in_specs = [
        pl.BlockSpec((1, tokens, block), functools.partial(lambda m, g, o, p: (p[m], 0, o[g]), m))
        for m in range(count)
    ] + [
        pl.BlockSpec((1, tokens, width), functools.partial(lambda m, g, o, p: (p[m], 0, 0), m))
        for m in range(count)
    ]
    out = pl.pallas_call(
        functools.partial(token_kernel, count=count),
        out_shape=jax.ShapeDtypeStruct((steps, block, width), jnp.float32),
        grid_spec=pltpu.PrefetchScalarGridSpec(
            num_scalar_prefetch=2,
            grid=(steps,),
            in_specs=in_specs,
            out_specs=pl.BlockSpec((1, block, width), lambda g, o, p: (g, 0, 0)),
        ),
        compiler_params=params(),
        cost_estimate=pl.CostEstimate(
            flops=2 * steps * block * width * count * tokens,
            bytes_accessed=steps * block * (count * tokens * 2 + width * 4),
            transcendentals=0,
        ),
    )(order, picks, *([acts] * count), *([grads] * count))
    return out.reshape(steps * block // rows, rows, width)


def key_kernel(place, current_ref, *refs, count):
    out_ref = refs[-1]
    for n in range(count):

        @pl.when(pl.program_id(0) == n)
        def _():
            out_ref[...] = lax.dot_general(
                current_ref[...], refs[n][...], (((1,), (1,)), ((), ())), preferred_element_type=jnp.float32
            ).astype(out_ref.dtype)


def key_products(place, current, parts, features, held):
    tokens, width = current.shape
    rows = parts[0].shape[0]
    count = len(parts)
    in_specs = [pl.BlockSpec((tokens, width), lambda g, p: (0, 0))] + [
        pl.BlockSpec((rows, width), lambda g, p: (0, 0)) for _ in parts
    ]
    operands = [place, current, *parts]
    aliases = {}
    if held is not None:
        in_specs.append(pl.BlockSpec(memory_space=pl.ANY))
        aliases = {len(operands): 0}
        operands.append(held)
    return pl.pallas_call(
        functools.partial(key_kernel, count=count),
        out_shape=jax.ShapeDtypeStruct((tokens, features), jnp.bfloat16),
        grid_spec=pltpu.PrefetchScalarGridSpec(
            num_scalar_prefetch=1,
            grid=(count,),
            in_specs=in_specs,
            out_specs=pl.BlockSpec((tokens, rows), lambda g, p: (0, p[g])),
        ),
        input_output_aliases=aliases,
        compiler_params=params(),
        cost_estimate=pl.CostEstimate(
            flops=2 * count * rows * width * tokens,
            bytes_accessed=2 * count * rows * (width + tokens),
            transcendentals=0,
        ),
    )(*operands)


def decode_kernel(place, *refs, count, rows, width, block):
    out_ref = refs[-1]
    slabs = width // LANES
    start = pl.multiple_of(pl.program_id(1) * block, block)
    for n in range(count):

        @pl.when(pl.program_id(0) == n)
        def _():
            scale = scale_of(refs[n], slabs * rows)
            for j in range(slabs):
                out_ref[0, :, j * LANES : (j + 1) * LANES] = decoded(
                    refs[n], pl.multiple_of(j * rows + start, block), block, scale
                )


def decode(place, codes, blocks, rows, width, held):
    count = len(codes)
    block = min(rows, 512)
    shape = code_shape(rows, width).shape
    in_specs = [pl.BlockSpec(shape, lambda g, s, p: (0, 0)) for _ in codes]
    operands = [place, *codes]
    aliases = {}
    if held is not None:
        in_specs.append(pl.BlockSpec(memory_space=pl.ANY))
        aliases = {len(operands): 0}
        operands.append(held)
    return pl.pallas_call(
        functools.partial(decode_kernel, count=count, rows=rows, width=width, block=block),
        out_shape=jax.ShapeDtypeStruct((blocks, rows, width), jnp.float32),
        grid_spec=pltpu.PrefetchScalarGridSpec(
            num_scalar_prefetch=1,
            grid=(count, rows // block),
            in_specs=in_specs,
            out_specs=pl.BlockSpec((1, block, width), lambda g, s, p: (p[g], s, 0)),
        ),
        input_output_aliases=aliases,
        compiler_params=params(),
        cost_estimate=pl.CostEstimate(
            flops=4 * count * rows * width, bytes_accessed=6 * count * rows * width, transcendentals=0
        ),
    )(*operands)


def body(acts, key_grads, weights, b_slot, cycle):
    stored, grads, weight = acts[0, 0], key_grads[0, 0], weights[0]
    slot = b_slot[0]
    micro, tokens, features = stored.shape
    width = grads.shape[2]
    n_dp, n_ctx = lax.axis_size("dp"), lax.axis_size("ctx")
    n_pipe = lax.axis_size("pipe")
    outer = n_dp // INNER
    replica, section = lax.axis_index("dp"), lax.axis_index("ctx")
    me_o, me_i = replica // INNER, replica % INNER
    groups = n_dp * n_ctx
    rows = features // groups
    pieces = cycle.shape[0]

    def swap(value):
        pairs = [(d, d // INNER * INNER + (d + 1) % INNER) for d in range(n_dp)]
        return lax.ppermute(value, "dp", pairs)

    def to_outer(value, by):
        return lax.ppermute(value, "dp", [(d, (d + by * INNER) % n_dp) for d in range(n_dp)])

    def to_ctx(value, by):
        return lax.ppermute(value, "ctx", [(d, (d + by) % n_ctx) for d in range(n_ctx)])

    def to_previous(value):
        return lax.ppermute(value, "pipe", [(d, d - 1) for d in range(1, n_pipe)])

    current = to_previous(lax.dynamic_index_in_dim(grads, slot, 0, keepdims=False))
    cuts = 2
    part = weight.shape[0] // (INNER * cuts)
    sent = [
        to_previous(lax.dynamic_slice_in_dim(weight, (me_i * cuts + c) * part, part, 0)) for c in range(cuts)
    ]

    position = jnp.arange(micro - 1, dtype=jnp.int32)
    picks = position + (position >= slot).astype(jnp.int32)
    block = min(rows, features // pieces, 512)
    piece_blocks = features // pieces // block
    blocks_of = rows // block

    def order_of(wanted):
        ids = []
        for kx, ko, ki in wanted:
            owner = ((section + kx) % n_ctx) * n_dp + ((me_o + ko) % outer) * INNER + (me_i + ki) % INNER
            at = owner * blocks_of + jnp.arange(blocks_of, dtype=jnp.int32)
            ids.append(cycle[at // piece_blocks] * piece_blocks + at % piece_blocks)
        return jnp.concatenate(ids)

    def products(wanted):
        return token_products(order_of(wanted), picks, stored, grads, block, rows)

    far = [(kx, ko) for ko in range(1, outer) for kx in range(1, n_ctx)]
    near = [(0, ko) for ko in range(1, outer)]
    home = [(kx, 0) for kx in range(n_ctx)]
    terms = {}
    for wanted in (far, near, home):
        theirs = swap(products([(*w, 1) for w in wanted]))
        mine = products([(*w, 0) for w in wanted])
        for n, w in enumerate(wanted):
            terms[w] = [(mine, n), (theirs, n)]

    got = {}
    for kx, ko in far + near:
        got[kx, ko] = to_outer(combine(terms[kx, ko], [], rows, width), ko)
    crossed = []
    for kx in range(1, n_ctx):
        value = combine(terms[kx, 0], [got[kx, ko] for ko in range(1, outer)], rows, width)
        crossed.append(to_ctx(value, kx))
    own = combine(terms[0, 0], [got[0, ko] for ko in range(1, outer)] + crossed, rows, width)
    result = decode(
        jnp.stack([me_o * INNER + me_i, me_o * INNER + (me_i + 1) % INNER]), [own, swap(own)], n_dp, rows, width, None
    )
    for ko in range(1, outer):
        other = to_outer(own, ko)
        o = (me_o - ko) % outer
        place = jnp.stack([o * INNER + me_i, o * INNER + (me_i + 1) % INNER])
        result = decode(place, [other, swap(other)], n_dp, rows, width, result)

    passed = None
    for kx in range(n_ctx):
        for c in range(cuts):
            held = sent[c] if kx == 0 else to_ctx(sent[c], kx)
            source = (section - kx) % n_ctx
            place = jnp.stack(
                [(source * INNER + me_i) * cuts + c, (source * INNER + (me_i + 1) % INNER) * cuts + c]
            )
            passed = key_products(place, current, [held, swap(held)], features, passed)
    return passed[None, None], result.reshape(1, n_dp * rows, width)


def solution(mesh):
    placed = (
        P("dp", "pipe", None, "ctx", None),
        P("dp", "pipe", None, "ctx", None),
        P("pipe", "ctx", None),
        P("pipe"),
        P(),
    )
    return jax.shard_map(
        body,
        mesh=mesh,
        in_specs=placed,
        out_specs=(P("dp", "pipe", "ctx", None), P("pipe", "ctx", None)),
        check_vma=False,
    )
```

```python
import functools
import math

import jax
import jax.numpy as jnp
from jax import lax
from jax.experimental import pallas as pl
from jax.experimental.pallas import tpu as pltpu
from jax.sharding import PartitionSpec as P

LANES = 128
TAIL = 16
MORE = 16
FAR_TAILS = 8
SIDE_TAILS = 6
DONE = jax.ShapeDtypeStruct((8, LANES), jnp.float32)
INNER = 2
TOP = 32767.0
VMEM_LIMIT = 48 << 20


def params():
    return pltpu.CompilerParams(vmem_limit_bytes=VMEM_LIMIT)


def code_shape(rows, width, tails=1):
    return jax.ShapeDtypeStruct((width // LANES * rows + TAIL * tails, LANES), jnp.int16)


def scale_of(code_ref, count):
    exponent = code_ref[count : count + TAIL, :].astype(jnp.int32)[0:1, :].astype(jnp.float32)
    return jnp.exp2(exponent) * (1.0 / (TOP * TOP))


def decoded(code_ref, start, rows, scale):
    level = code_ref[pl.ds(start, rows), :].astype(jnp.int32).astype(jnp.float32)
    return level * jnp.abs(level) * scale


def hold_kernel(*refs):
    pass


def after(value, *waits):
    return pl.pallas_call(
        hold_kernel,
        out_shape=jax.ShapeDtypeStruct(value.shape, value.dtype),
        in_specs=[pl.BlockSpec(memory_space=pl.ANY)] + [pl.BlockSpec(memory_space=pl.ANY) for _ in waits],
        out_specs=pl.BlockSpec(memory_space=pl.ANY),
        input_output_aliases={0: 0},
        compiler_params=params(),
    )(value, *waits)


def gather_total(total_ref, start, rows, whole, codes, largest):
    width = total_ref.shape[1]
    step = min(rows, 128)
    slabs = width // LANES
    scales = [scale_of(c, slabs * whole) for c in codes]

    def add(i, largest):
        r = pl.multiple_of(start + i * step, step)
        for j in range(slabs):
            slab = slice(j * LANES, (j + 1) * LANES)
            value = total_ref[pl.ds(r, step), slab]
            for c, scale in zip(codes, scales):
                value = value + decoded(c, pl.multiple_of(j * whole + r, step), step, scale)
            if codes:
                total_ref[pl.ds(r, step), slab] = value
            largest = jnp.maximum(largest, jnp.max(jnp.abs(value).reshape(step // 8, 8, LANES), axis=0))
        return largest

    return lax.fori_loop(0, rows // step, add, largest)


def encode(total_ref, largest, out_ref):
    rows, width = total_ref.shape
    step = min(rows, 128)
    slabs = width // LANES
    largest = jnp.max(jnp.max(largest, axis=0, keepdims=True), axis=1, keepdims=True)
    exponent = jnp.floor(jnp.log2(jnp.maximum(largest, 1e-30))) + 2.0
    exponent = jnp.broadcast_to(exponent, (8, LANES))
    shrink = jnp.exp2(-exponent)[0:1, :]

    def one(i, carry):
        r = pl.multiple_of(i * step, step)
        for j in range(slabs):
            value = total_ref[pl.ds(r, step), j * LANES : (j + 1) * LANES]
            root = jnp.round(jnp.sqrt(jnp.abs(value) * shrink) * TOP)
            level = jnp.where(value < 0.0, -root, root)
            place = pl.ds(pl.multiple_of(j * rows + r, step), step)
            out_ref[place, :] = level.astype(jnp.int32).astype(jnp.int16)
        return carry

    lax.fori_loop(0, rows // step, one, 0)
    tail = jnp.concatenate([exponent] * ((out_ref.shape[0] - slabs * rows) // 8), axis=0)
    out_ref[slabs * rows :, :] = tail.astype(jnp.int32).astype(jnp.int16)


def combine_kernel(kept_ref, *refs, n_codes, rows):
    out_ref, total_ref = refs[-2:]
    total_ref[...] = kept_ref[0]
    largest = gather_total(total_ref, 0, rows, rows, refs[:n_codes], jnp.zeros((8, LANES), jnp.float32))
    encode(total_ref, largest, out_ref)


def combine(kept, at, codes, *waits, tails=1):
    _, rows, width = kept.shape
    shape = code_shape(rows, width, tails)
    in_specs = (
        [pl.BlockSpec((1, rows, width), lambda i: (at, 0, 0))]
        + [pl.BlockSpec(x.shape, lambda i: (0, 0)) for x in codes]
        + [pl.BlockSpec(memory_space=pl.ANY) for _ in waits]
    )
    return pl.pallas_call(
        functools.partial(combine_kernel, n_codes=len(codes), rows=rows),
        out_shape=shape,
        grid=(1,),
        in_specs=in_specs,
        out_specs=pl.BlockSpec(shape.shape, lambda i: (0, 0)),
        scratch_shapes=[pltpu.VMEM((rows, width), jnp.float32)],
        compiler_params=params(),
    )(kept, *codes, *waits)


def token_kernel(order, picks, starts, *refs, count, groups, n_codes, n_waits, moves, n_sources, coded, rows, block):
    left = jnp.concatenate([r[0] for r in refs[:count]], axis=0)
    right = jnp.concatenate([r[0] for r in refs[count : 2 * count]], axis=0)
    refs = refs[2 * count :]
    codes, sources, outs = refs[:n_codes], refs[n_codes : n_codes + n_sources], refs[n_codes + n_sources + n_waits :]
    step = pl.program_id(1)
    ends = (pl.program_id(0) == groups - 1) & (step == rows // block - 1)
    copies = []
    n_out = groups if coded else 1
    for n, segments in enumerate(moves):
        place = 0
        for source, length in segments:
            at = pl.ds(pl.multiple_of(starts[len(copies)], TAIL), length)
            to = outs[n_out + n].at[pl.ds(place, length), :]
            copies.append((sources[source].at[at, :], to, outs[-1].at[len(copies)]))
            place += length
    if copies:

        @pl.when((pl.program_id(0) == 0) & (step == 0))
        def _():
            for c in copies:
                pltpu.make_async_copy(*c).start()

    product = lax.dot_general(left, right, (((0,), (0,)), ((), ())), preferred_element_type=jnp.float32)
    start = pl.multiple_of(step * block, block)
    scratch = outs[n_out + len(moves) :]
    total_ref = scratch[0] if coded else outs[0].at[0]
    total_ref[pl.ds(start, block), :] = product
    each = n_codes // groups
    for n in range(groups if coded or codes else 0):

        @pl.when(pl.program_id(0) == n)
        def _():
            seen = jnp.zeros((8, LANES), jnp.float32)
            if coded:
                largest_ref = scratch[1]
                seen = jnp.where(step == 0, seen, largest_ref[...])
            seen = gather_total(total_ref, start, block, rows, codes[n * each : (n + 1) * each], seen)
            if coded:
                largest_ref[...] = seen

                @pl.when(step == rows // block - 1)
                def _():
                    encode(total_ref, largest_ref[...], outs[n])

    if copies:

        @pl.when(ends)
        def _():
            for c in copies:
                pltpu.make_async_copy(*c).wait()


def token_products(
    order, first, groups, picks, acts, grads, block, rows, coded, codes, *waits, tails=1, sources=(), moves=()
):
    count = picks.shape[0]
    tokens = acts.shape[1]
    width = grads.shape[2]
    steps = rows // block
    shape = code_shape(rows, width, tails)
    in_specs = (
        [
            pl.BlockSpec(
                (1, tokens, block),
                functools.partial(lambda m, g, s, o, p, q: (p[m], 0, o[first + g * steps + s]), m),
            )
            for m in range(count)
        ]
        + [
            pl.BlockSpec((1, tokens, width), functools.partial(lambda m, g, s, o, p, q: (p[m], 0, 0), m))
            for m in range(count)
        ]
        + [pl.BlockSpec(x.shape, lambda g, s, o, p, q: (0, 0)) for x in codes]
        + [pl.BlockSpec(memory_space=pltpu.HBM) for _ in sources]
        + [pl.BlockSpec(memory_space=pl.ANY) for _ in waits]
    )
    if coded:
        out_shape = [shape] * groups
        out_specs = [pl.BlockSpec(shape.shape, lambda g, s, o, p, q: (0, 0))] * groups
        scratch = [pltpu.VMEM((rows, width), jnp.float32), pltpu.VMEM((8, LANES), jnp.float32)]
    else:
        out_shape = [jax.ShapeDtypeStruct((groups, rows, width), jnp.float32)]
        out_specs = [pl.BlockSpec((1, rows, width), lambda g, s, o, p, q: (g, 0, 0))]
        scratch = []
    starts = [jnp.asarray(at, jnp.int32) for m in moves for _, at, _ in m]
    for m in moves:
        like = sources[m[0][0]]
        out_shape.append(jax.ShapeDtypeStruct((sum(n for _, _, n in m), like.shape[1]), like.dtype))
        out_specs.append(pl.BlockSpec(out_shape[-1].shape, lambda g, s, o, p, q: (0, 0)))
    if moves:
        scratch.append(pltpu.SemaphoreType.DMA((len(starts),)))
    return pl.pallas_call(
        functools.partial(
            token_kernel,
            count=count,
            groups=groups,
            n_codes=len(codes),
            n_waits=len(waits),
            moves=[[(source, n) for source, _, n in m] for m in moves],
            n_sources=len(sources),
            coded=coded,
            rows=rows,
            block=block,
        ),
        out_shape=out_shape,
        grid_spec=pltpu.PrefetchScalarGridSpec(
            num_scalar_prefetch=3, grid=(groups, steps), in_specs=in_specs, out_specs=out_specs, scratch_shapes=scratch
        ),
        compiler_params=params(),
    )(
        order,
        picks,
        jnp.stack(starts) if starts else picks,
        *([acts] * count),
        *([grads] * count),
        *codes,
        *sources,
        *waits,
    )


def key_kernel(starts, current_ref, *refs, count, skip, rows):
    out_ref, done_ref, block_ref, sem = refs[-4:]
    step = min(rows, 512)
    copies = []
    for n in range(count):
        place = pl.multiple_of(starts[n], LANES)
        for at in range(0, rows, step):
            size = min(step, rows - at)
            block_ref[n, :, at : at + size] = lax.dot_general(
                current_ref[...],
                refs[n][skip + at : skip + at + size, :],
                (((1,), (1,)), ((), ())),
                preferred_element_type=jnp.float32,
            ).astype(out_ref.dtype)
        copies.append(pltpu.make_async_copy(block_ref.at[n], out_ref.at[:, pl.ds(place, rows)], sem.at[n]))
        copies[-1].start()
    done_ref[...] = jnp.zeros_like(done_ref)
    for c in copies:
        c.wait()


def key_products(starts, current, parts, skip, rows, features, held, *waits):
    tokens, width = current.shape
    count = len(parts)
    anywhere = pl.BlockSpec(memory_space=pltpu.HBM)
    in_specs = [pl.BlockSpec(x.shape, lambda i, p: (0, 0)) for x in (current, *parts)]
    operands = [starts, current, *parts]
    aliases = {}
    if held is not None:
        in_specs.append(anywhere)
        aliases = {len(operands): 0}
        operands.append(held)
    in_specs += [pl.BlockSpec(memory_space=pl.ANY) for _ in waits]
    operands += waits
    return pl.pallas_call(
        functools.partial(key_kernel, count=count, skip=skip, rows=rows),
        out_shape=[jax.ShapeDtypeStruct((tokens, features), jnp.bfloat16), DONE],
        grid_spec=pltpu.PrefetchScalarGridSpec(
            num_scalar_prefetch=1,
            grid=(1,),
            in_specs=in_specs,
            out_specs=[anywhere, pl.BlockSpec(DONE.shape, lambda i, p: (0, 0))],
            scratch_shapes=[pltpu.VMEM((count, tokens, rows), jnp.bfloat16), pltpu.SemaphoreType.DMA((count,))],
        ),
        input_output_aliases=aliases,
        compiler_params=params(),
    )(*operands)


def decode_kernel(place, *refs, count, rows, width):
    out_ref, done_ref, block_ref, sem = refs[-4:]
    slabs = width // LANES
    step = min(rows, 128)
    copies = []
    for n in range(count):
        scale = scale_of(refs[n], slabs * rows)

        def one(i, carry):
            r = pl.multiple_of(i * step, step)
            for j in range(slabs):
                block_ref[n, pl.ds(r, step), j * LANES : (j + 1) * LANES] = decoded(
                    refs[n], pl.multiple_of(j * rows + r, step), step, scale
                )
            return carry

        for k in range(2):
            part = rows // 2
            lax.fori_loop(k * part // step, (k + 1) * part // step, one, 0)
            at = pl.ds(k * part, part)
            copies.append(
                pltpu.make_async_copy(block_ref.at[n, at, :], out_ref.at[place[n], at, :], sem.at[2 * n + k])
            )
            copies[-1].start()
    done_ref[...] = jnp.zeros_like(done_ref)
    for c in copies:
        c.wait()


def decode(place, codes, blocks, rows, width, held, *waits):
    count = len(codes)
    anywhere = pl.BlockSpec(memory_space=pltpu.HBM)
    in_specs = [pl.BlockSpec(x.shape, lambda i, p: (0, 0)) for x in codes]
    operands = [place, *codes]
    aliases = {}
    if held is not None:
        in_specs.append(anywhere)
        aliases = {len(operands): 0}
        operands.append(held)
    in_specs += [pl.BlockSpec(memory_space=pl.ANY) for _ in waits]
    operands += waits
    return pl.pallas_call(
        functools.partial(decode_kernel, count=count, rows=rows, width=width),
        out_shape=[jax.ShapeDtypeStruct((blocks, rows, width), jnp.float32), DONE],
        grid_spec=pltpu.PrefetchScalarGridSpec(
            num_scalar_prefetch=1,
            grid=(1,),
            in_specs=in_specs,
            out_specs=[anywhere, pl.BlockSpec(DONE.shape, lambda i, p: (0, 0))],
            scratch_shapes=[
                pltpu.VMEM((count, rows, width), jnp.float32),
                pltpu.SemaphoreType.DMA((2 * count,)),
            ],
        ),
        input_output_aliases=aliases,
        compiler_params=params(),
    )(*operands)


def body(acts, key_grads, weights, b_slot, cycle):
    stored, grads, weight = acts[0, 0], key_grads[0, 0], weights[0]
    slot = b_slot[0]
    micro, tokens, features = stored.shape
    width = grads.shape[2]
    n_dp, n_ctx = lax.axis_size("dp"), lax.axis_size("ctx")
    n_pipe = lax.axis_size("pipe")
    outer = n_dp // INNER
    replica, section = lax.axis_index("dp"), lax.axis_index("ctx")
    me_o, me_i = replica // INNER, replica % INNER
    groups = n_dp * n_ctx
    rows = features // groups
    pieces = cycle.shape[0]

    def swap(value):
        pairs = [(d, d // INNER * INNER + (d + 1) % INNER) for d in range(n_dp)]
        return lax.ppermute(value, "dp", pairs)

    def to_outer(value, by):
        return lax.ppermute(value, "dp", [(d, (d + by * INNER) % n_dp) for d in range(n_dp)])

    def to_ctx(value, by):
        return lax.ppermute(value, "ctx", [(d, (d + by) % n_ctx) for d in range(n_ctx)])

    def to_previous(value):
        return lax.ppermute(value, "pipe", [(d, d - 1) for d in range(1, n_pipe)])

    half = weight.shape[0] // INNER
    part = half // 2
    late_part = max(half * 3 // 8 // LANES, 1) * LANES

    position = jnp.arange(micro - 1, dtype=jnp.int32)
    picks = position + (position >= slot).astype(jnp.int32)
    block = min(rows, features // pieces, 512)
    piece_blocks = features // pieces // block
    blocks_of = rows // block
    far = [(kx, ko) for ko in range(1, outer) for kx in range(1, n_ctx)]
    near = [(0, ko) for ko in range(1, outer)]
    side = [(kx, 0) for kx in range(1, n_ctx)]
    home = [(0, 0)]
    order, first, at = [], {}, 0
    for name, wanted, ki in (
        ("far", far, 1),
        ("far", far, 0),
        ("near side", near + side, 1),
        ("near", near, 0),
        ("side", side, 0),
        ("home", home, 1),
        ("home", home, 0),
    ):
        first[name, ki] = at
        for kx, ko in wanted:
            owner = ((section + kx) % n_ctx) * n_dp + ((me_o + ko) % outer) * INNER + (me_i + ki) % INNER
            order.append(owner * blocks_of + jnp.arange(blocks_of, dtype=jnp.int32))
            at += blocks_of
    order = jnp.concatenate(order)
    order = cycle[order // piece_blocks] * piece_blocks + order % piece_blocks

    def products(name, ki, wanted, coded, codes, *waits, **more):
        return token_products(
            order, first[name, ki], len(wanted), picks, stored, grads, block, rows, coded, codes, *waits, **more
        )

    *far_sent, own_first, own_most, own_second = products(
        "far",
        1,
        far,
        True,
        [],
        sources=(weight, grads.reshape(micro * tokens, width)),
        moves=(
            [(0, me_i * half, part), (1, slot * tokens, tokens)],
            [(0, me_i * half + late_part - MORE, half - late_part + MORE)],
            [(0, me_i * half + part - MORE, half - part + MORE)],
        ),
    )
    z_first = to_previous(own_first)
    crossed_most = [to_ctx(own_most, kx) for kx in range(1, n_ctx)]
    coded = dict(zip(far, products("far", 0, far, True, [swap(c) for c in far_sent], tails=FAR_TAILS)))
    got = {w: to_outer(coded[w], w[1]) for w in far}
    sent = products("near side", 1, near + side, True, [], *coded.values())
    theirs = [swap(c) for c in sent]
    coded = dict(zip(near, products("near", 0, near, True, theirs[: len(near)], tails=SIDE_TAILS)))
    (side_sums,) = products("side", 0, side, False, theirs[len(near) :], *coded.values())
    got.update({w: to_outer(after(coded[w], *[got[f] for f in far]), w[1]) for w in near})

    passed = passed_done = None

    def pass_on(kx, start, count, held, skip, *waits):
        nonlocal passed, passed_done
        row = ((section - kx) % n_ctx) * weight.shape[0] + start
        starts = jnp.stack([row + me_i * half, row + (me_i + 1) % INNER * half])
        passed, passed_done = key_products(starts, current, [held, swap(held)], skip, count, features, passed, *waits)

    crossed = []
    for n, (kx, _) in enumerate(side):
        value = combine(side_sums, n, [got[kx, ko] for ko in range(1, outer)], tails=SIDE_TAILS)
        crossed.append(to_ctx(value, kx))
    z_second = to_previous(after(own_second, z_first, side_sums, *crossed_most, *[got[w] for w in far]))
    home_theirs = swap(products("home", 1, home, True, [], value)[0])
    (home_sum,) = products("home", 0, home, False, [home_theirs])
    current = lax.slice_in_dim(z_first, part, part + tokens)
    next_first = lax.slice_in_dim(z_first, 0, part)
    next_late = lax.slice_in_dim(z_first, 0, late_part)
    pass_on(0, 0, part, next_first, 0, home_sum)
    z_crossed = [to_previous(after(c, z_second)) for c in crossed_most]
    own = combine(home_sum, 0, [got[0, ko] for ko in range(1, outer)] + crossed, z_second, passed_done, next_late, tails=2)
    others = {ko: to_outer(own, ko) for ko in range(1, outer)}
    late = after(next_late, own)
    late = [to_ctx(late, kx) for kx in range(1, n_ctx)]
    result, result_done = decode(
        jnp.stack([me_o * INNER + me_i, me_o * INNER + (me_i + 1) % INNER]),
        [own, swap(own)],
        n_dp,
        rows,
        width,
        None,
    )
    pass_on(0, part, half - part, after(z_second, own), MORE, result_done)
    early_done = passed_done
    for kx in range(1, n_ctx):
        pass_on(kx, late_part, half - late_part, z_crossed[kx - 1], MORE)
    most_done = passed_done
    for kx in range(1, n_ctx):
        pass_on(kx, 0, late_part, late[kx - 1], 0)
    for ko in range(1, outer):
        other = after(others[ko], early_done)
        o = (me_o - ko) % outer
        place = jnp.stack([o * INNER + me_i, o * INNER + (me_i + 1) % INNER])
        result, _ = decode(place, [other, swap(other)], n_dp, rows, width, result, most_done)
    return passed[None, None], result.reshape(1, n_dp * rows, width)


def solution(mesh):
    placed = (
        P("dp", "pipe", None, "ctx", None),
        P("dp", "pipe", None, "ctx", None),
        P("pipe", "ctx", None),
        P("pipe"),
        P(),
    )
    return jax.shard_map(
        body,
        mesh=mesh,
        in_specs=placed,
        out_specs=(P("dp", "pipe", "ctx", None), P("pipe", "ctx", None)),
        check_vma=False,
    )
```

```python
import functools
import math

import jax
import jax.numpy as jnp
from jax import lax
from jax.experimental import pallas as pl
from jax.experimental.pallas import tpu as pltpu
from jax.sharding import PartitionSpec as P

LANES = 128
TAIL = 16
FAR_TAILS = 8
SIDE_TAILS = 6
DONE = jax.ShapeDtypeStruct((8, LANES), jnp.float32)
INNER = 2
TOP = 32767.0
VMEM_LIMIT = 48 << 20


def params():
    return pltpu.CompilerParams(vmem_limit_bytes=VMEM_LIMIT)


def code_shape(rows, width, tails=1):
    return jax.ShapeDtypeStruct((width // LANES * rows + TAIL * tails, LANES), jnp.int16)


def scale_of(code_ref, count):
    exponent = code_ref[count : count + TAIL, :].astype(jnp.int32)[0:1, :].astype(jnp.float32)
    return jnp.exp2(exponent) * (1.0 / (TOP * TOP))


def decoded(code_ref, start, rows, scale):
    level = code_ref[pl.ds(start, rows), :].astype(jnp.int32).astype(jnp.float32)
    return level * jnp.abs(level) * scale


def hold_kernel(*refs):
    pass


def after(value, *waits):
    return pl.pallas_call(
        hold_kernel,
        out_shape=jax.ShapeDtypeStruct(value.shape, value.dtype),
        in_specs=[pl.BlockSpec(memory_space=pl.ANY)] + [pl.BlockSpec(memory_space=pl.ANY) for _ in waits],
        out_specs=pl.BlockSpec(memory_space=pl.ANY),
        input_output_aliases={0: 0},
        compiler_params=params(),
    )(value, *waits)


def gather_total(total_ref, start, rows, whole, codes, largest):
    width = total_ref.shape[1]
    step = min(rows, 128)
    slabs = width // LANES
    scales = [scale_of(c, slabs * whole) for c in codes]

    def add(i, largest):
        r = pl.multiple_of(start + i * step, step)
        for j in range(slabs):
            slab = slice(j * LANES, (j + 1) * LANES)
            value = total_ref[pl.ds(r, step), slab]
            for c, scale in zip(codes, scales):
                value = value + decoded(c, pl.multiple_of(j * whole + r, step), step, scale)
            if codes:
                total_ref[pl.ds(r, step), slab] = value
            largest = jnp.maximum(largest, jnp.max(jnp.abs(value).reshape(step // 8, 8, LANES), axis=0))
        return largest

    return lax.fori_loop(0, rows // step, add, largest)


def encode(total_ref, largest, out_ref):
    rows, width = total_ref.shape
    step = min(rows, 128)
    slabs = width // LANES
    largest = jnp.max(jnp.max(largest, axis=0, keepdims=True), axis=1, keepdims=True)
    exponent = jnp.floor(jnp.log2(jnp.maximum(largest, 1e-30))) + 2.0
    exponent = jnp.broadcast_to(exponent, (8, LANES))
    shrink = jnp.exp2(-exponent)[0:1, :]

    def one(i, carry):
        r = pl.multiple_of(i * step, step)
        for j in range(slabs):
            value = total_ref[pl.ds(r, step), j * LANES : (j + 1) * LANES]
            root = jnp.round(jnp.sqrt(jnp.abs(value) * shrink) * TOP)
            level = jnp.where(value < 0.0, -root, root)
            place = pl.ds(pl.multiple_of(j * rows + r, step), step)
            out_ref[place, :] = level.astype(jnp.int32).astype(jnp.int16)
        return carry

    lax.fori_loop(0, rows // step, one, 0)
    tail = jnp.concatenate([exponent] * ((out_ref.shape[0] - slabs * rows) // 8), axis=0)
    out_ref[slabs * rows :, :] = tail.astype(jnp.int32).astype(jnp.int16)


def combine_kernel(kept_ref, *refs, n_codes, rows):
    out_ref, total_ref = refs[-2:]
    total_ref[...] = kept_ref[0]
    largest = gather_total(total_ref, 0, rows, rows, refs[:n_codes], jnp.zeros((8, LANES), jnp.float32))
    encode(total_ref, largest, out_ref)


def combine(kept, at, codes, *waits, tails=1):
    _, rows, width = kept.shape
    shape = code_shape(rows, width, tails)
    in_specs = (
        [pl.BlockSpec((1, rows, width), lambda i: (at, 0, 0))]
        + [pl.BlockSpec(x.shape, lambda i: (0, 0)) for x in codes]
        + [pl.BlockSpec(memory_space=pl.ANY) for _ in waits]
    )
    return pl.pallas_call(
        functools.partial(combine_kernel, n_codes=len(codes), rows=rows),
        out_shape=shape,
        grid=(1,),
        in_specs=in_specs,
        out_specs=pl.BlockSpec(shape.shape, lambda i: (0, 0)),
        scratch_shapes=[pltpu.VMEM((rows, width), jnp.float32)],
        compiler_params=params(),
    )(kept, *codes, *waits)


def token_kernel(order, picks, starts, *refs, count, groups, n_codes, n_waits, moves, n_sources, coded, rows, block):
    left = jnp.concatenate([r[0] for r in refs[:count]], axis=0)
    right = jnp.concatenate([r[0] for r in refs[count : 2 * count]], axis=0)
    refs = refs[2 * count :]
    codes, sources, outs = refs[:n_codes], refs[n_codes : n_codes + n_sources], refs[n_codes + n_sources + n_waits :]
    step = pl.program_id(1)
    ends = (pl.program_id(0) == groups - 1) & (step == rows // block - 1)
    copies = []
    n_out = groups if coded else 1
    for n, segments in enumerate(moves):
        place = 0
        for source, length in segments:
            at = pl.ds(pl.multiple_of(starts[len(copies)], TAIL), length)
            to = outs[n_out + n].at[pl.ds(place, length), :]
            copies.append((sources[source].at[at, :], to, outs[-1].at[len(copies)]))
            place += length
    if copies:

        @pl.when((pl.program_id(0) == 0) & (step == 0))
        def _():
            for c in copies:
                pltpu.make_async_copy(*c).start()

    product = lax.dot_general(left, right, (((0,), (0,)), ((), ())), preferred_element_type=jnp.float32)
    start = pl.multiple_of(step * block, block)
    scratch = outs[n_out + len(moves) :]
    total_ref = scratch[0] if coded else outs[0].at[0]
    total_ref[pl.ds(start, block), :] = product
    each = n_codes // groups
    for n in range(groups if coded or codes else 0):

        @pl.when(pl.program_id(0) == n)
        def _():
            seen = jnp.zeros((8, LANES), jnp.float32)
            if coded:
                largest_ref = scratch[1]
                seen = jnp.where(step == 0, seen, largest_ref[...])
            seen = gather_total(total_ref, start, block, rows, codes[n * each : (n + 1) * each], seen)
            if coded:
                largest_ref[...] = seen

                @pl.when(step == rows // block - 1)
                def _():
                    encode(total_ref, largest_ref[...], outs[n])

    if copies:

        @pl.when(ends)
        def _():
            for c in copies:
                pltpu.make_async_copy(*c).wait()


def token_products(
    order, first, groups, picks, acts, grads, block, rows, coded, codes, *waits, tails=1, sources=(), moves=()
):
    count = picks.shape[0]
    tokens = acts.shape[1]
    width = grads.shape[2]
    steps = rows // block
    shape = code_shape(rows, width, tails)
    in_specs = (
        [
            pl.BlockSpec(
                (1, tokens, block),
                functools.partial(lambda m, g, s, o, p, q: (p[m], 0, o[first + g * steps + s]), m),
            )
            for m in range(count)
        ]
        + [
            pl.BlockSpec((1, tokens, width), functools.partial(lambda m, g, s, o, p, q: (p[m], 0, 0), m))
            for m in range(count)
        ]
        + [pl.BlockSpec(x.shape, lambda g, s, o, p, q: (0, 0)) for x in codes]
        + [pl.BlockSpec(memory_space=pltpu.HBM) for _ in sources]
        + [pl.BlockSpec(memory_space=pl.ANY) for _ in waits]
    )
    if coded:
        out_shape = [shape] * groups
        out_specs = [pl.BlockSpec(shape.shape, lambda g, s, o, p, q: (0, 0))] * groups
        scratch = [pltpu.VMEM((rows, width), jnp.float32), pltpu.VMEM((8, LANES), jnp.float32)]
    else:
        out_shape = [jax.ShapeDtypeStruct((groups, rows, width), jnp.float32)]
        out_specs = [pl.BlockSpec((1, rows, width), lambda g, s, o, p, q: (g, 0, 0))]
        scratch = []
    starts = [jnp.asarray(at, jnp.int32) for m in moves for _, at, _ in m]
    for m in moves:
        like = sources[m[0][0]]
        out_shape.append(jax.ShapeDtypeStruct((sum(n for _, _, n in m), like.shape[1]), like.dtype))
        out_specs.append(pl.BlockSpec(out_shape[-1].shape, lambda g, s, o, p, q: (0, 0)))
    if moves:
        scratch.append(pltpu.SemaphoreType.DMA((len(starts),)))
    return pl.pallas_call(
        functools.partial(
            token_kernel,
            count=count,
            groups=groups,
            n_codes=len(codes),
            n_waits=len(waits),
            moves=[[(source, n) for source, _, n in m] for m in moves],
            n_sources=len(sources),
            coded=coded,
            rows=rows,
            block=block,
        ),
        out_shape=out_shape,
        grid_spec=pltpu.PrefetchScalarGridSpec(
            num_scalar_prefetch=3, grid=(groups, steps), in_specs=in_specs, out_specs=out_specs, scratch_shapes=scratch
        ),
        compiler_params=params(),
    )(
        order,
        picks,
        jnp.stack(starts) if starts else picks,
        *([acts] * count),
        *([grads] * count),
        *codes,
        *sources,
        *waits,
    )


def key_kernel(starts, current_ref, *refs, segments):
    out_ref, done_ref = refs[len(refs) - len(segments) - 3 : len(refs) - len(segments) - 1]
    blocks, sem = refs[len(refs) - len(segments) - 1 : -1], refs[-1]
    copies = []
    for n, (skip, rows) in enumerate(segments):
        step = min(rows, 512)
        for at in range(0, rows, step):
            size = min(step, rows - at)
            blocks[n][:, at : at + size] = lax.dot_general(
                current_ref[...],
                refs[n][skip + at : skip + at + size, :],
                (((1,), (1,)), ((), ())),
                preferred_element_type=jnp.float32,
            ).astype(out_ref.dtype)
        place = pl.ds(pl.multiple_of(starts[n], LANES), rows)
        copies.append(pltpu.make_async_copy(blocks[n], out_ref.at[:, place], sem.at[n]))
        copies[-1].start()
    done_ref[...] = jnp.zeros_like(done_ref)
    for c in copies:
        c.wait()


def key_products(current, parts, features, held, *waits):
    tokens, width = current.shape
    arrays = [x for x, _, _, _ in parts]
    anywhere = pl.BlockSpec(memory_space=pltpu.HBM)
    in_specs = [pl.BlockSpec(x.shape, lambda i, p: (0, 0)) for x in (current, *arrays)]
    operands = [jnp.stack([start for _, _, _, start in parts]), current, *arrays]
    aliases = {}
    if held is not None:
        in_specs.append(anywhere)
        aliases = {len(operands): 0}
        operands.append(held)
    in_specs += [pl.BlockSpec(memory_space=pl.ANY) for _ in waits]
    operands += waits
    return pl.pallas_call(
        functools.partial(key_kernel, segments=[(skip, rows) for _, skip, rows, _ in parts]),
        out_shape=[jax.ShapeDtypeStruct((tokens, features), jnp.bfloat16), DONE],
        grid_spec=pltpu.PrefetchScalarGridSpec(
            num_scalar_prefetch=1,
            grid=(1,),
            in_specs=in_specs,
            out_specs=[anywhere, pl.BlockSpec(DONE.shape, lambda i, p: (0, 0))],
            scratch_shapes=[pltpu.VMEM((tokens, rows), jnp.bfloat16) for _, _, rows, _ in parts]
            + [pltpu.SemaphoreType.DMA((len(parts),))],
        ),
        input_output_aliases=aliases,
        compiler_params=params(),
    )(*operands)


def decode_kernel(place, *refs, count, rows, width):
    out_ref, done_ref, block_ref, sem = refs[-4:]
    slabs = width // LANES
    step = min(rows, 128)
    copies = []
    for n in range(count):
        scale = scale_of(refs[n], slabs * rows)

        def one(i, carry):
            r = pl.multiple_of(i * step, step)
            for j in range(slabs):
                block_ref[n, pl.ds(r, step), j * LANES : (j + 1) * LANES] = decoded(
                    refs[n], pl.multiple_of(j * rows + r, step), step, scale
                )
            return carry

        for k in range(2):
            part = rows // 2
            lax.fori_loop(k * part // step, (k + 1) * part // step, one, 0)
            at = pl.ds(k * part, part)
            copies.append(
                pltpu.make_async_copy(block_ref.at[n, at, :], out_ref.at[place[n], at, :], sem.at[2 * n + k])
            )
            copies[-1].start()
    done_ref[...] = jnp.zeros_like(done_ref)
    for c in copies:
        c.wait()


def decode(place, codes, blocks, rows, width, held, *waits):
    count = len(codes)
    anywhere = pl.BlockSpec(memory_space=pltpu.HBM)
    in_specs = [pl.BlockSpec(x.shape, lambda i, p: (0, 0)) for x in codes]
    operands = [place, *codes]
    aliases = {}
    if held is not None:
        in_specs.append(anywhere)
        aliases = {len(operands): 0}
        operands.append(held)
    in_specs += [pl.BlockSpec(memory_space=pl.ANY) for _ in waits]
    operands += waits
    return pl.pallas_call(
        functools.partial(decode_kernel, count=count, rows=rows, width=width),
        out_shape=[jax.ShapeDtypeStruct((blocks, rows, width), jnp.float32), DONE],
        grid_spec=pltpu.PrefetchScalarGridSpec(
            num_scalar_prefetch=1,
            grid=(1,),
            in_specs=in_specs,
            out_specs=[anywhere, pl.BlockSpec(DONE.shape, lambda i, p: (0, 0))],
            scratch_shapes=[
                pltpu.VMEM((count, rows, width), jnp.float32),
                pltpu.SemaphoreType.DMA((2 * count,)),
            ],
        ),
        input_output_aliases=aliases,
        compiler_params=params(),
    )(*operands)


def body(acts, key_grads, weights, b_slot, cycle):
    stored, grads, weight = acts[0, 0], key_grads[0, 0], weights[0]
    slot = b_slot[0]
    micro, tokens, features = stored.shape
    width = grads.shape[2]
    n_dp, n_ctx = lax.axis_size("dp"), lax.axis_size("ctx")
    n_pipe = lax.axis_size("pipe")
    outer = n_dp // INNER
    replica, section = lax.axis_index("dp"), lax.axis_index("ctx")
    me_o, me_i = replica // INNER, replica % INNER
    groups = n_dp * n_ctx
    rows = features // groups
    pieces = cycle.shape[0]

    def swap(value):
        pairs = [(d, d // INNER * INNER + (d + 1) % INNER) for d in range(n_dp)]
        return lax.ppermute(value, "dp", pairs)

    def to_outer(value, by):
        return lax.ppermute(value, "dp", [(d, (d + by * INNER) % n_dp) for d in range(n_dp)])

    def to_ctx(value, by):
        return lax.ppermute(value, "ctx", [(d, (d + by) % n_ctx) for d in range(n_ctx)])

    def to_previous(value):
        return lax.ppermute(value, "pipe", [(d, d - 1) for d in range(1, n_pipe)])

    half = weight.shape[0] // INNER
    late_part = max(half * 3 // 8 // LANES, 1) * LANES

    position = jnp.arange(micro - 1, dtype=jnp.int32)
    picks = position + (position >= slot).astype(jnp.int32)
    block = min(rows, features // pieces, 512)
    piece_blocks = features // pieces // block
    blocks_of = rows // block
    far = [(kx, ko) for ko in range(1, outer) for kx in range(1, n_ctx)]
    near = [(0, ko) for ko in range(1, outer)]
    side = [(kx, 0) for kx in range(1, n_ctx)]
    home = [(0, 0)]
    order, first, at = [], {}, 0
    for name, wanted, ki in (
        ("far", far, 1),
        ("far", far, 0),
        ("near side", near + side, 1),
        ("near", near, 0),
        ("side", side, 0),
        ("home", home, 1),
        ("home", home, 0),
    ):
        first[name, ki] = at
        for kx, ko in wanted:
            owner = ((section + kx) % n_ctx) * n_dp + ((me_o + ko) % outer) * INNER + (me_i + ki) % INNER
            order.append(owner * blocks_of + jnp.arange(blocks_of, dtype=jnp.int32))
            at += blocks_of
    order = jnp.concatenate(order)
    order = cycle[order // piece_blocks] * piece_blocks + order % piece_blocks

    def products(name, ki, wanted, coded, codes, *waits, **more):
        return token_products(
            order, first[name, ki], len(wanted), picks, stored, grads, block, rows, coded, codes, *waits, **more
        )

    *far_sent, own_all, own_most = products(
        "far",
        1,
        far,
        True,
        [],
        sources=(weight, grads.reshape(micro * tokens, width)),
        moves=(
            [(0, me_i * half, half), (1, slot * tokens, tokens)],
            [(0, me_i * half + late_part, half - late_part)],
        ),
    )
    z_all = to_previous(own_all)
    crossed_most = [to_ctx(own_most, kx) for kx in range(1, n_ctx)]
    coded = dict(zip(far, products("far", 0, far, True, [swap(c) for c in far_sent], tails=FAR_TAILS)))
    got = {w: to_outer(coded[w], w[1]) for w in far}
    sent = products("near side", 1, near + side, True, [], *coded.values())
    theirs = [swap(c) for c in sent]
    coded = dict(zip(near, products("near", 0, near, True, theirs[: len(near)], tails=SIDE_TAILS)))
    (side_sums,) = products("side", 0, side, False, theirs[len(near) :], *coded.values())
    got.update({w: to_outer(after(coded[w], *[got[f] for f in far]), w[1]) for w in near})

    passed = passed_done = None

    def pass_on(kx, start, count, held, skip, *waits, cuts=1):
        nonlocal passed, passed_done
        row = ((section - kx) % n_ctx) * weight.shape[0] + start
        parts = [(held, skip, count, row + me_i * half)]
        theirs = row + (me_i + 1) % INNER * half
        if cuts == 1:
            parts.append((swap(held), skip, count, theirs))
        at = 0
        while cuts > 1 and at < count:
            size = min(-(-count // cuts // LANES) * LANES, count - at)
            parts.append((swap(lax.slice_in_dim(held, skip + at, skip + at + size)), 0, size, theirs + at))
            at += size
        passed, passed_done = key_products(current, parts, features, passed, *waits)

    crossed = []
    for n, (kx, _) in enumerate(side):
        value = combine(side_sums, n, [got[kx, ko] for ko in range(1, outer)], *crossed_most, tails=SIDE_TAILS)
        crossed.append(to_ctx(value, kx))
    home_sent = products("home", 1, home, True, [], value)
    home_theirs = swap(home_sent[0])
    (home_sum,) = products("home", 0, home, False, [home_theirs])
    z_crossed = [to_previous(after(c, home_sent[0])) for c in crossed_most]
    current = lax.slice_in_dim(z_all, half, half + tokens)
    next_late = lax.slice_in_dim(z_all, 0, late_part)
    codes = [*[got[0, ko] for ko in range(1, outer)], *crossed]
    own = combine(home_sum, 0, codes, current, next_late, tails=2)
    others = {ko: to_outer(own, ko) for ko in range(1, outer)}
    late = after(next_late, own)
    late = [to_ctx(late, kx) for kx in range(1, n_ctx)]
    result, result_done = decode(
        jnp.stack([me_o * INNER + me_i, me_o * INNER + (me_i + 1) % INNER]),
        [own, swap(own)],
        n_dp,
        rows,
        width,
        None,
    )
    pass_on(0, 0, half, after(z_all, own), 0, result_done, cuts=2)
    early_done = passed_done
    for kx in range(1, n_ctx):
        pass_on(kx, late_part, half - late_part, after(z_crossed[kx - 1], early_done), 0, cuts=2)
    theirs = []
    for ko in range(1, outer):
        other = after(others[ko], passed_done, result_done, *late)
        theirs.append(swap(other))
        o = (me_o - ko) % outer
        place = jnp.stack([o * INNER + me_i, o * INNER + (me_i + 1) % INNER])
        result, _ = decode(place, [other, theirs[-1]], n_dp, rows, width, result)
    for kx in range(1, n_ctx):
        pass_on(kx, 0, late_part, after(late[kx - 1], *theirs), 0)
    return passed[None, None], result.reshape(1, n_dp * rows, width)


def solution(mesh):
    placed = (
        P("dp", "pipe", None, "ctx", None),
        P("dp", "pipe", None, "ctx", None),
        P("pipe", "ctx", None),
        P("pipe"),
        P(),
    )
    return jax.shard_map(
        body,
        mesh=mesh,
        in_specs=placed,
        out_specs=(P("dp", "pipe", "ctx", None), P("pipe", "ctx", None)),
        check_vma=False,
    )
```

```python
import functools
import math

import jax
import jax.numpy as jnp
from jax import lax
from jax.experimental import pallas as pl
from jax.experimental.pallas import tpu as pltpu
from jax.sharding import PartitionSpec as P

LANES = 128
TAIL = 16
MORE = 16
FAR_TAILS = 3
SIDE_TAILS = 6
DONE = jax.ShapeDtypeStruct((8, LANES), jnp.float32)
INNER = 2
TOP = 32767.0
VMEM_LIMIT = 26 << 20
TOKEN_VMEM_LIMIT = 48 << 20
FIRST_VMEM_LIMIT = 48 << 20


def params(limit=VMEM_LIMIT):
    return pltpu.CompilerParams(vmem_limit_bytes=limit)


def code_shape(rows, width, tails=1):
    return jax.ShapeDtypeStruct((width // LANES * rows + TAIL * tails, LANES), jnp.int16)


def scale_of(code_ref, count):
    exponent = code_ref[count : count + TAIL, :].astype(jnp.int32)[0:1, :].astype(jnp.float32)
    return jnp.exp2(exponent) * (1.0 / (TOP * TOP))


def decoded(code_ref, start, rows, scale):
    level = code_ref[pl.ds(start, rows), :].astype(jnp.int32).astype(jnp.float32)
    return level * jnp.abs(level) * scale


def hold_kernel(*refs):
    pass


def after(value, *waits):
    return pl.pallas_call(
        hold_kernel,
        out_shape=jax.ShapeDtypeStruct(value.shape, value.dtype),
        in_specs=[pl.BlockSpec(memory_space=pl.ANY)] + [pl.BlockSpec(memory_space=pl.ANY) for _ in waits],
        out_specs=pl.BlockSpec(memory_space=pl.ANY),
        input_output_aliases={0: 0},
        compiler_params=params(),
    )(value, *waits)


def split_kernel(value_ref, *refs, cuts):
    outs, buffers, sem = refs[: len(cuts)], refs[len(cuts) : -1], refs[-1]
    coming = [
        pltpu.make_async_copy(value_ref.at[pl.ds(at, rows), :], buffers[n], sem.at[n])
        for n, (at, rows) in enumerate(cuts)
    ]
    leaving = [
        pltpu.make_async_copy(buffers[n], outs[n], sem.at[len(cuts) + n]) for n in range(len(cuts))
    ]
    for c in coming:
        c.start()
    for c, d in zip(coming, leaving):
        c.wait()
        d.start()
    for d in leaving:
        d.wait()


def split(value, *cuts):
    shapes = [jax.ShapeDtypeStruct((rows, value.shape[1]), value.dtype) for _, rows in cuts]
    return pl.pallas_call(
        functools.partial(split_kernel, cuts=cuts),
        out_shape=shapes,
        in_specs=[pl.BlockSpec(memory_space=pl.ANY)],
        out_specs=[pl.BlockSpec(memory_space=pl.ANY)] * len(cuts),
        scratch_shapes=[pltpu.VMEM(x.shape, x.dtype) for x in shapes]
        + [pltpu.SemaphoreType.DMA((2 * len(cuts),))],
        compiler_params=params(),
    )(value)


def gather_total(total_ref, start, rows, whole, codes, largest):
    width = total_ref.shape[1]
    step = min(rows, 128)
    slabs = width // LANES
    scales = [scale_of(c, slabs * whole) for c in codes]

    def add(i, largest):
        r = pl.multiple_of(start + i * step, step)
        for j in range(slabs):
            slab = slice(j * LANES, (j + 1) * LANES)
            value = total_ref[pl.ds(r, step), slab]
            for c, scale in zip(codes, scales):
                value = value + decoded(c, pl.multiple_of(j * whole + r, step), step, scale)
            if codes:
                total_ref[pl.ds(r, step), slab] = value
            largest = jnp.maximum(largest, jnp.max(jnp.abs(value).reshape(step // 8, 8, LANES), axis=0))
        return largest

    return lax.fori_loop(0, rows // step, add, largest)


def encode(total_ref, largest, out_ref):
    rows, width = total_ref.shape
    step = min(rows, 128)
    slabs = width // LANES
    largest = jnp.max(jnp.max(largest, axis=0, keepdims=True), axis=1, keepdims=True)
    exponent = jnp.floor(jnp.log2(jnp.maximum(largest, 1e-30))) + 2.0
    exponent = jnp.broadcast_to(exponent, (8, LANES))
    shrink = jnp.exp2(-exponent)[0:1, :]

    def one(i, carry):
        r = pl.multiple_of(i * step, step)
        for j in range(slabs):
            value = total_ref[pl.ds(r, step), j * LANES : (j + 1) * LANES]
            root = jnp.round(jnp.sqrt(jnp.abs(value) * shrink) * TOP)
            level = jnp.where(value < 0.0, -root, root)
            place = pl.ds(pl.multiple_of(j * rows + r, step), step)
            out_ref[place, :] = level.astype(jnp.int32).astype(jnp.int16)
        return carry

    lax.fori_loop(0, rows // step, one, 0)
    tail = jnp.concatenate([exponent] * ((out_ref.shape[0] - slabs * rows) // 8), axis=0)
    out_ref[slabs * rows :, :] = tail.astype(jnp.int32).astype(jnp.int16)


def combine_kernel(kept_ref, *refs, n_codes, rows):
    out_ref, total_ref = refs[-2:]
    total_ref[...] = kept_ref[0]
    largest = gather_total(total_ref, 0, rows, rows, refs[:n_codes], jnp.zeros((8, LANES), jnp.float32))
    encode(total_ref, largest, out_ref)


def combine(kept, codes, *waits, tails=1):
    _, rows, width = kept.shape
    shape = code_shape(rows, width, tails)
    in_specs = (
        [pl.BlockSpec((1, rows, width), lambda i: (0, 0, 0))]
        + [pl.BlockSpec(x.shape, lambda i: (0, 0)) for x in codes]
        + [pl.BlockSpec(memory_space=pl.ANY) for _ in waits]
    )
    return pl.pallas_call(
        functools.partial(combine_kernel, n_codes=len(codes), rows=rows),
        out_shape=shape,
        grid=(1,),
        in_specs=in_specs,
        out_specs=pl.BlockSpec(shape.shape, lambda i: (0, 0)),
        scratch_shapes=[pltpu.VMEM((rows, width), jnp.float32)],
        compiler_params=params(),
    )(kept, *codes, *waits)


def token_kernel(where, slot, cycle, acts_ref, grads_ref, *refs, owners, sizes, n_codes, n_sources, n_waits, coded, moves, rows, block):
    codes, sources, refs = refs[:n_codes], refs[n_codes : n_codes + n_sources], refs[n_codes + n_sources + n_waits :]
    groups = len(owners)
    outs, moved, refs = refs[:groups], refs[groups : groups + len(moves)], refs[groups + len(moves) :]
    left_ref, right_ref, total_refs, code_refs, sem = refs[:5]
    moving_refs = refs[5:]
    count, tokens = acts_ref.shape[0] - 1, grads_ref.shape[1]
    steps = rows // block
    n_ctx, outer, piece = sizes
    copies = []

    def copy(source, target):
        copies.append(pltpu.make_async_copy(source, target, sem.at[len(copies)]))
        copies[-1].start()
        return copies[-1]

    def pick(m):
        return m + (m >= slot[0]).astype(jnp.int32)

    def first_column(k):
        kx, ko, ki = owners[k // steps]
        ctx = lax.rem(where[0] + kx, n_ctx)
        replica = lax.rem(where[1] + ko, outer) * INNER + lax.rem(where[2] + ki, INNER)
        at = (ctx * (outer * INNER) + replica) * rows + k % steps * block
        return pl.multiple_of(cycle[at // piece] * piece + lax.rem(at, piece), block)

    ready = []
    for k in range(groups * steps):
        ready.append([])
        columns = pl.ds(first_column(k), block)
        for m in range(count):
            place = pl.ds(m * tokens, tokens)
            if k == 0:
                ready[0].append(copy(grads_ref.at[pick(m)], right_ref.at[place, :]))
            ready[k].append(copy(acts_ref.at[pick(m), :, columns], left_ref.at[k, place, :]))
    moving = []
    for buffer_ref, segments in zip(moving_refs, moves):
        place = 0
        for source, start, length in segments:
            there = pl.ds(pl.multiple_of(start(where, slot), TAIL), length)
            moving.append(copy(sources[source].at[there, :], buffer_ref.at[pl.ds(place, length), :]))
            place += length

    each = n_codes // groups
    leaving = []
    for n in range(groups):
        total_ref = total_refs.at[n]
        largest = jnp.zeros((8, LANES), jnp.float32)
        for b in range(steps):
            k = n * steps + b
            for c in ready[k]:
                c.wait()
            part = pl.ds(b * block, block)
            total_ref[part, :] = lax.dot_general(
                left_ref[k], right_ref[...], (((0,), (0,)), ((), ())), preferred_element_type=jnp.float32
            )
            if coded[n] or codes:
                largest = gather_total(total_ref, b * block, block, rows, codes[n * each : (n + 1) * each], largest)
            if not coded[n]:
                leaving.append(copy(total_ref.at[part, :], outs[n].at[0, part, :]))
        if coded[n]:
            encode(total_ref, largest, code_refs.at[n])
            leaving.append(copy(code_refs.at[n], outs[n]))
        if n == 0:
            for c in moving:
                c.wait()
            leaving += [copy(buffer_ref, out_ref) for buffer_ref, out_ref in zip(moving_refs, moved)]
    for c in leaving:
        c.wait()


def token_products(
    where, slot, cycle, sizes, owners, coded, acts, grads, block, rows, codes, *waits, tails=1, sources=(), moves=(), limit
):
    count = acts.shape[0] - 1
    tokens = acts.shape[1]
    width = grads.shape[2]
    groups = len(owners)
    blocks = groups * (rows // block)
    shape = code_shape(rows, width, tails)

    stays = pl.BlockSpec(memory_space=pltpu.HBM)
    in_specs = (
        [stays, stays]
        + [pl.BlockSpec(x.shape, lambda i, *_: (0, 0)) for x in codes]
        + [stays for _ in sources]
        + [pl.BlockSpec(memory_space=pl.ANY) for _ in waits]
    )
    out_shape = [shape if c else jax.ShapeDtypeStruct((1, rows, width), jnp.float32) for c in coded]
    for m in moves:
        like = sources[m[0][0]]
        out_shape.append(jax.ShapeDtypeStruct((sum(n for _, _, n in m), like.shape[1]), like.dtype))
    n_copies = count * (blocks + 1) + sum(len(m) + 1 for m in moves) + blocks
    scratch = [
        pltpu.VMEM((blocks, count * tokens, block), acts.dtype),
        pltpu.VMEM((count * tokens, width), grads.dtype),
        pltpu.VMEM((groups, rows, width), jnp.float32),
        pltpu.VMEM((groups if any(coded) else 1, *(shape.shape if any(coded) else (TAIL, LANES))), jnp.int16),
        pltpu.SemaphoreType.DMA((n_copies,)),
    ] + [pltpu.VMEM(x.shape, x.dtype) for x in out_shape[groups:]]
    return pl.pallas_call(
        functools.partial(
            token_kernel,
            owners=owners,
            sizes=sizes,
            n_codes=len(codes),
            n_sources=len(sources),
            n_waits=len(waits),
            coded=coded,
            moves=moves,
            rows=rows,
            block=block,
        ),
        out_shape=out_shape,
        grid_spec=pltpu.PrefetchScalarGridSpec(
            num_scalar_prefetch=3,
            grid=(1,),
            in_specs=in_specs,
            out_specs=[pl.BlockSpec(memory_space=pl.ANY) for _ in out_shape],
            scratch_shapes=scratch,
        ),
        compiler_params=params(limit),
    )(where, slot, cycle, acts, grads, *codes, *sources, *waits)


def key_kernel(starts, current_ref, *refs, segments):
    out_ref, done_ref = refs[len(refs) - len(segments) - 3 : len(refs) - len(segments) - 1]
    blocks, sem = refs[len(refs) - len(segments) - 1 : -1], refs[-1]
    copies = []
    for n, (skip, rows) in enumerate(segments):
        step = min(rows, 512)
        for at in range(0, rows, step):
            size = min(step, rows - at)
            blocks[n][:, at : at + size] = lax.dot_general(
                current_ref[...],
                refs[n][skip + at : skip + at + size, :],
                (((1,), (1,)), ((), ())),
                preferred_element_type=jnp.float32,
            ).astype(out_ref.dtype)
        place = pl.ds(pl.multiple_of(starts[n], LANES), rows)
        copies.append(pltpu.make_async_copy(blocks[n], out_ref.at[:, place], sem.at[n]))
        copies[-1].start()
    done_ref[...] = jnp.zeros_like(done_ref)
    for c in copies:
        c.wait()


def key_products(current, parts, features, held, *waits):
    tokens, width = current.shape
    arrays = [x for x, _, _, _ in parts]
    anywhere = pl.BlockSpec(memory_space=pltpu.HBM)
    in_specs = [pl.BlockSpec(x.shape, lambda i, p: (0, 0)) for x in (current, *arrays)]
    operands = [jnp.stack([start for _, _, _, start in parts]), current, *arrays]
    aliases = {}
    if held is not None:
        in_specs.append(anywhere)
        aliases = {len(operands): 0}
        operands.append(held)
    in_specs += [pl.BlockSpec(memory_space=pl.ANY) for _ in waits]
    operands += waits
    return pl.pallas_call(
        functools.partial(key_kernel, segments=[(skip, rows) for _, skip, rows, _ in parts]),
        out_shape=[jax.ShapeDtypeStruct((tokens, features), jnp.bfloat16), DONE],
        grid_spec=pltpu.PrefetchScalarGridSpec(
            num_scalar_prefetch=1,
            grid=(1,),
            in_specs=in_specs,
            out_specs=[anywhere, pl.BlockSpec(DONE.shape, lambda i, p: (0, 0))],
            scratch_shapes=[pltpu.VMEM((tokens, rows), jnp.bfloat16) for _, _, rows, _ in parts]
            + [pltpu.SemaphoreType.DMA((len(parts),))],
        ),
        input_output_aliases=aliases,
        compiler_params=params(),
    )(*operands)


def decode_kernel(place, *refs, count, rows, width):
    out_ref, done_ref, code_refs, block_ref, sem = refs[-5:]
    slabs = width // LANES
    step = min(rows, 128)
    coming = [pltpu.make_async_copy(refs[n], code_refs.at[n], sem.at[n]) for n in range(count)]
    for c in coming:
        c.start()
    copies = []
    for n in range(count):
        coming[n].wait()
        scale = scale_of(code_refs.at[n], slabs * rows)

        def one(i, carry):
            r = pl.multiple_of(i * step, step)
            for j in range(slabs):
                block_ref[n, pl.ds(r, step), j * LANES : (j + 1) * LANES] = decoded(
                    code_refs.at[n], pl.multiple_of(j * rows + r, step), step, scale
                )
            return carry

        for k in range(2):
            part = rows // 2
            lax.fori_loop(k * part // step, (k + 1) * part // step, one, 0)
            at = pl.ds(k * part, part)
            copies.append(
                pltpu.make_async_copy(
                    block_ref.at[n, at, :], out_ref.at[place[n], at, :], sem.at[count + 2 * n + k]
                )
            )
            copies[-1].start()
    done_ref[...] = jnp.zeros_like(done_ref)
    for c in copies:
        c.wait()


def decode(place, codes, blocks, rows, width, held, *waits):
    count = len(codes)
    anywhere = pl.BlockSpec(memory_space=pltpu.HBM)
    in_specs = [pl.BlockSpec(memory_space=pl.ANY) for _ in codes]
    operands = [place, *codes]
    aliases = {}
    if held is not None:
        in_specs.append(anywhere)
        aliases = {len(operands): 0}
        operands.append(held)
    in_specs += [pl.BlockSpec(memory_space=pl.ANY) for _ in waits]
    operands += waits
    return pl.pallas_call(
        functools.partial(decode_kernel, count=count, rows=rows, width=width),
        out_shape=[jax.ShapeDtypeStruct((blocks, rows, width), jnp.float32), DONE],
        grid_spec=pltpu.PrefetchScalarGridSpec(
            num_scalar_prefetch=1,
            grid=(1,),
            in_specs=in_specs,
            out_specs=[anywhere, pl.BlockSpec(DONE.shape, lambda i, p: (0, 0))],
            scratch_shapes=[
                pltpu.VMEM((count, *codes[0].shape), jnp.int16),
                pltpu.VMEM((count, rows, width), jnp.float32),
                pltpu.SemaphoreType.DMA((3 * count,)),
            ],
        ),
        input_output_aliases=aliases,
        compiler_params=params(),
    )(*operands)


def body(acts, key_grads, weights, b_slot, cycle):
    stored, grads, weight = acts[0, 0], key_grads[0, 0], weights[0]
    micro, tokens, features = stored.shape
    width = grads.shape[2]
    n_dp, n_ctx = lax.axis_size("dp"), lax.axis_size("ctx")
    n_pipe = lax.axis_size("pipe")
    outer = n_dp // INNER
    replica, section = lax.axis_index("dp"), lax.axis_index("ctx")
    me_o, me_i = replica // INNER, replica % INNER
    groups = n_dp * n_ctx
    rows = features // groups
    pieces = cycle.shape[0]

    def swap(value):
        pairs = [(d, d // INNER * INNER + (d + 1) % INNER) for d in range(n_dp)]
        return lax.ppermute(value, "dp", pairs)

    def to_outer(value, by):
        return lax.ppermute(value, "dp", [(d, (d + by * INNER) % n_dp) for d in range(n_dp)])

    def to_ctx(value, by):
        return lax.ppermute(value, "ctx", [(d, (d + by) % n_ctx) for d in range(n_ctx)])

    def to_previous(value):
        return lax.ppermute(value, "pipe", [(d, d - 1) for d in range(1, n_pipe)])

    half = weight.shape[0] // INNER
    late_part = max(half * 3 // 8 // LANES, 1) * LANES

    block = min(rows, features // pieces, 512)
    far = [(kx, ko) for ko in range(1, outer) for kx in range(1, n_ctx)]
    near = [(0, ko) for ko in range(1, outer)]
    side = [(kx, 0) for kx in range(1, n_ctx)]
    home = [(0, 0)]
    where = jnp.stack([section, me_o, me_i]).astype(jnp.int32)
    sizes = (n_ctx, outer, features // pieces)

    def sent_by(wanted):
        return [(kx, ko, 1) for kx, ko in wanted]

    def kept_by(wanted):
        return [(kx, ko, 0) for kx, ko in wanted]

    def products(owners, coded, codes, *waits, limit=TOKEN_VMEM_LIMIT, **more):
        flags = coded if isinstance(coded, list) else [coded] * len(owners)
        return token_products(
            where, b_slot, cycle, sizes, owners, flags, stored, grads, block, rows, codes, *waits, limit=limit, **more
        )

    *far_out, own_all, own_most = products(
        sent_by(far) + kept_by(far),
        [True] * len(far) + [False] * len(far),
        [],
        sources=(weight, grads.reshape(micro * tokens, width)),
        moves=(
            [(0, lambda w, b: w[2] * half, half), (1, lambda w, b: b[0] * tokens, tokens)],
            [(0, lambda w, b: w[2] * half + late_part, half - late_part)],
        ),
        limit=FIRST_VMEM_LIMIT,
    )
    z_all = to_previous(own_all)
    crossed_most = [to_ctx(own_most, kx) for kx in range(1, n_ctx)]
    far_theirs = [swap(c) for c in far_out[: len(far)]]
    coded = {
        w: combine(kept, [theirs], tails=FAR_TAILS) for w, kept, theirs in zip(far, far_out[len(far) :], far_theirs)
    }
    got = {w: to_outer(coded[w], w[1]) for w in far}
    sent = products(sent_by(near + side), True, [], *coded.values())
    theirs = [swap(c) for c in sent]
    coded = dict(zip(near, products(kept_by(near), True, theirs[: len(near)], tails=SIDE_TAILS)))
    side_sums = products(kept_by(side), False, theirs[len(near) :], *coded.values())

    passed = passed_done = None

    def pass_on(kx, start, pieces, *waits):
        nonlocal passed, passed_done
        parts = []
        for piece, rows in pieces:
            row = ((section - kx) % n_ctx) * weight.shape[0] + start
            parts.append((piece, 0, rows, row + me_i * half))
            parts.append((swap(piece), 0, rows, row + (me_i + 1) % INNER * half))
            start = start + rows
        passed, passed_done = key_products(current, parts, features, passed, *waits)
        return [x for x, _, _, _ in parts[1::2]]

    values = [
        combine(total, [got[kx, ko] for ko in range(1, outer)], tails=SIDE_TAILS + 1)
        for (kx, _), total in zip(side, side_sums)
    ]
    crossed = [to_ctx(v, kx) for (kx, _), v in zip(side, values)]
    got.update({w: to_outer(after(coded[w], *values), w[1]) for w in near})
    home_sent = products(sent_by(home), True, [], *values, *crossed_most)
    home_theirs = swap(home_sent[0])
    (home_kept,) = products(kept_by(home), False, [], home_sent[0])
    z_crossed = [to_previous(after(c, home_kept)) for c in crossed_most]
    z_first, z_second, late, current = split(
        z_all,
        (0, half // 2 + MORE),
        (half // 2, half - half // 2 + MORE),
        (0, late_part),
        (half, tokens),
    )
    z_pieces = [(z_first, half // 2), (z_second, half - half // 2)]
    codes = [home_theirs, *[got[0, ko] for ko in range(1, outer)], *crossed]
    own = combine(home_kept, codes, current, tails=2)
    others = {ko: to_outer(own, ko) for ko in range(1, outer)}
    late = [to_ctx(late, kx) for kx in range(1, n_ctx)]
    pass_on(0, 0, z_pieces)
    result, result_done = decode(
        jnp.stack([me_o * INNER + me_i, me_o * INNER + (me_i + 1) % INNER]),
        [own, swap(own)],
        n_dp,
        rows,
        width,
        None,
        passed_done,
    )
    most = half - late_part
    first = min(-(-most * 11 // 16 // LANES) * LANES, most - LANES)
    for kx in range(1, n_ctx):
        held = after(z_crossed[kx - 1], result_done)
        pieces = split(held, (0, first), (first, most - first))
        pass_on(kx, late_part, [(pieces[0], first), (pieces[1], most - first)])
    crossed_done = passed_done
    late_theirs = []
    for kx in range(1, n_ctx):
        late_theirs += pass_on(kx, 0, [(late[kx - 1], late_part)])
    for ko in range(1, outer):
        other = after(others[ko], crossed_done, *late_theirs)
        o = (me_o - ko) % outer
        place = jnp.stack([o * INNER + me_i, o * INNER + (me_i + 1) % INNER])
        result, _ = decode(place, [other, swap(other)], n_dp, rows, width, result, passed_done)
    return passed[None, None], result.reshape(1, n_dp * rows, width)


def solution(mesh):
    placed = (
        P("dp", "pipe", None, "ctx", None),
        P("dp", "pipe", None, "ctx", None),
        P("pipe", "ctx", None),
        P("pipe"),
        P(),
    )
    return jax.shard_map(
        body,
        mesh=mesh,
        in_specs=placed,
        out_specs=(P("dp", "pipe", "ctx", None), P("pipe", "ctx", None)),
        check_vma=False,
    )
```

```python
import functools
import math

import jax
import jax.numpy as jnp
from jax import lax
from jax.experimental import pallas as pl
from jax.experimental.pallas import tpu as pltpu
from jax.sharding import PartitionSpec as P

LANES = 128
TAIL = 16
CHUNKS = 2
MORE = 32
PAD = 160
LATE_PAD = 48
FAR_TAILS = 3
SIDE_TAILS = 16
DONE = jax.ShapeDtypeStruct((8, LANES), jnp.float32)
INNER = 2
TOP = 32767.0
VMEM_LIMIT = 26 << 20
TOKEN_VMEM_LIMIT = 47 << 20
FIRST_VMEM_LIMIT = 47 << 20


def params(limit=VMEM_LIMIT):
    return pltpu.CompilerParams(vmem_limit_bytes=limit)


def code_shape(rows, width, tails=1):
    return jax.ShapeDtypeStruct((width // LANES * rows + TAIL * tails, LANES), jnp.int16)


def scale_of(code_ref, count):
    exponent = code_ref[count : count + TAIL, :].astype(jnp.int32)[0:1, :].astype(jnp.float32)
    return jnp.exp2(exponent) * (1.0 / (TOP * TOP))


def decoded(code_ref, start, rows, scale):
    level = code_ref[pl.ds(start, rows), :].astype(jnp.int32).astype(jnp.float32)
    return level * jnp.abs(level) * scale


def hold_kernel(*refs):
    pass


def after(value, *waits):
    return pl.pallas_call(
        hold_kernel,
        out_shape=jax.ShapeDtypeStruct(value.shape, value.dtype),
        in_specs=[pl.BlockSpec(memory_space=pl.ANY)] + [pl.BlockSpec(memory_space=pl.ANY) for _ in waits],
        out_specs=pl.BlockSpec(memory_space=pl.ANY),
        input_output_aliases={0: 0},
        compiler_params=params(),
    )(value, *waits)


def split_kernel(value_ref, *refs, cuts):
    outs, buffers, sem = refs[: len(cuts)], refs[len(cuts) : -1], refs[-1]
    coming = [
        pltpu.make_async_copy(value_ref.at[pl.ds(at, rows), :], buffers[n], sem.at[n])
        for n, (at, rows) in enumerate(cuts)
    ]
    leaving = [
        pltpu.make_async_copy(buffers[n], outs[n], sem.at[len(cuts) + n]) for n in range(len(cuts))
    ]
    for c in coming:
        c.start()
    for c, d in zip(coming, leaving):
        c.wait()
        d.start()
    for d in leaving:
        d.wait()


def split(value, *cuts):
    shapes = [jax.ShapeDtypeStruct((rows, value.shape[1]), value.dtype) for _, rows in cuts]
    return pl.pallas_call(
        functools.partial(split_kernel, cuts=cuts),
        out_shape=shapes,
        in_specs=[pl.BlockSpec(memory_space=pl.ANY)],
        out_specs=[pl.BlockSpec(memory_space=pl.ANY)] * len(cuts),
        scratch_shapes=[pltpu.VMEM(x.shape, x.dtype) for x in shapes]
        + [pltpu.SemaphoreType.DMA((2 * len(cuts),))],
        compiler_params=params(),
    )(value)


def gather_total(total_ref, start, rows, whole, codes, largest):
    width = total_ref.shape[1]
    step = min(rows, 128)
    slabs = width // LANES
    scales = [scale_of(c, slabs * whole) for c in codes]

    def add(i, largest):
        r = pl.multiple_of(start + i * step, step)
        for j in range(slabs):
            slab = slice(j * LANES, (j + 1) * LANES)
            value = total_ref[pl.ds(r, step), slab]
            for c, scale in zip(codes, scales):
                value = value + decoded(c, pl.multiple_of(r * slabs + j * step, step), step, scale)
            if codes:
                total_ref[pl.ds(r, step), slab] = value
            largest = jnp.maximum(largest, jnp.max(jnp.abs(value).reshape(step // 8, 8, LANES), axis=0))
        return largest

    return lax.fori_loop(0, rows // step, add, largest)


def encode(total_ref, largest, out_ref):
    rows, width = total_ref.shape
    step = min(rows, 128)
    slabs = width // LANES
    largest = jnp.max(jnp.max(largest, axis=0, keepdims=True), axis=1, keepdims=True)
    exponent = jnp.floor(jnp.log2(jnp.maximum(largest, 1e-30))) + 2.0
    exponent = jnp.broadcast_to(exponent, (8, LANES))
    shrink = jnp.exp2(-exponent)[0:1, :]

    def one(i, carry):
        r = pl.multiple_of(i * step, step)
        for j in range(slabs):
            value = total_ref[pl.ds(r, step), j * LANES : (j + 1) * LANES]
            root = jnp.round(jnp.sqrt(jnp.abs(value) * shrink) * TOP)
            level = jnp.where(value < 0.0, -root, root)
            place = pl.ds(pl.multiple_of(r * slabs + j * step, step), step)
            out_ref[place, :] = level.astype(jnp.int32).astype(jnp.int16)
        return carry

    lax.fori_loop(0, rows // step, one, 0)
    tail = jnp.concatenate([exponent] * ((out_ref.shape[0] - slabs * rows) // 8), axis=0)
    out_ref[slabs * rows :, :] = tail.astype(jnp.int32).astype(jnp.int16)


def combine_kernel(kept_ref, *refs, n_codes, rows):
    out_ref, total_ref = refs[-2:]
    total_ref[...] = kept_ref[0]
    largest = gather_total(total_ref, 0, rows, rows, refs[:n_codes], jnp.zeros((8, LANES), jnp.float32))
    encode(total_ref, largest, out_ref)


def combine(kept, codes, *waits, tails=1):
    _, rows, width = kept.shape
    shape = code_shape(rows, width, tails)
    in_specs = (
        [pl.BlockSpec((1, rows, width), lambda i: (0, 0, 0))]
        + [pl.BlockSpec(x.shape, lambda i: (0, 0)) for x in codes]
        + [pl.BlockSpec(memory_space=pl.ANY) for _ in waits]
    )
    return pl.pallas_call(
        functools.partial(combine_kernel, n_codes=len(codes), rows=rows),
        out_shape=shape,
        grid=(1,),
        in_specs=in_specs,
        out_specs=pl.BlockSpec(shape.shape, lambda i: (0, 0)),
        scratch_shapes=[pltpu.VMEM((rows, width), jnp.float32)],
        compiler_params=params(),
    )(kept, *codes, *waits)


def token_kernel(
    where,
    slot,
    cycle,
    acts_ref,
    grads_ref,
    *refs,
    owners,
    sizes,
    n_codes,
    n_sources,
    n_waits,
    coded,
    moves,
    rows,
    block,
):
    codes, sources, refs = refs[:n_codes], refs[n_codes : n_codes + n_sources], refs[n_codes + n_sources + n_waits :]
    groups = len(owners)
    outs, moved, refs = refs[:groups], refs[groups : groups + len(moves)], refs[groups + len(moves) :]
    left_ref, right_ref, total_refs, code_refs, sem = refs[:5]
    moving_refs = refs[5:]
    count, tokens = acts_ref.shape[0] - 1, grads_ref.shape[1]
    steps = rows // block
    n_ctx, outer, piece = sizes
    copies = []

    def copy(source, target):
        copies.append(pltpu.make_async_copy(source, target, sem.at[len(copies)]))
        copies[-1].start()
        return copies[-1]

    def pick(m):
        return m + (m >= slot[0]).astype(jnp.int32)

    def first_column(k):
        kx, ko, ki = owners[k // steps]
        ctx = lax.rem(where[0] + kx, n_ctx)
        replica = lax.rem(where[1] + ko, outer) * INNER + lax.rem(where[2] + ki, INNER)
        at = (ctx * (outer * INNER) + replica) * rows + k % steps * block
        return pl.multiple_of(cycle[at // piece] * piece + lax.rem(at, piece), block)

    ready = []
    for k in range(groups * steps):
        ready.append([])
        columns = pl.ds(first_column(k), block)
        for m in range(count):
            place = pl.ds(m * tokens, tokens)
            if k == 0:
                ready[0].append(copy(grads_ref.at[pick(m)], right_ref.at[place, :]))
            ready[k].append(copy(acts_ref.at[pick(m), :, columns], left_ref.at[k, place, :]))
    moving = []
    for buffer_ref, segments in zip(moving_refs, moves):
        place = 0
        for source, start, length in segments:
            there = pl.ds(pl.multiple_of(start(where, slot), TAIL), length)
            moving.append(copy(sources[source].at[there, :], buffer_ref.at[pl.ds(place, length), :]))
            place += length

    each = n_codes // groups
    leaving = []
    for n in range(groups):
        total_ref = total_refs.at[n]
        largest = jnp.zeros((8, LANES), jnp.float32)
        for b in range(steps):
            k = n * steps + b
            for c in ready[k]:
                c.wait()
            part = pl.ds(b * block, block)
            total_ref[part, :] = lax.dot_general(
                left_ref[k], right_ref[...], (((0,), (0,)), ((), ())), preferred_element_type=jnp.float32
            )
            if coded[n] or codes:
                largest = gather_total(total_ref, b * block, block, rows, codes[n * each : (n + 1) * each], largest)
            if not coded[n]:
                leaving.append(copy(total_ref.at[part, :], outs[n].at[0, part, :]))
        if coded[n]:
            encode(total_ref, largest, code_refs.at[n])
            leaving.append(copy(code_refs.at[n], outs[n]))
        if n == 0:
            for c in moving:
                c.wait()
            leaving += [copy(buffer_ref, out_ref) for buffer_ref, out_ref in zip(moving_refs, moved)]
    for c in leaving:
        c.wait()


def token_products(
    where, slot, cycle, sizes, owners, coded, acts, grads, block, rows, codes, *waits, tails=1, sources=(), moves=(), limit
):
    count = acts.shape[0] - 1
    tokens = acts.shape[1]
    width = grads.shape[2]
    groups = len(owners)
    blocks = groups * (rows // block)
    shape = code_shape(rows, width, tails)

    stays = pl.BlockSpec(memory_space=pltpu.HBM)
    in_specs = (
        [stays, stays]
        + [pl.BlockSpec(x.shape, lambda i, *_: (0, 0)) for x in codes]
        + [stays for _ in sources]
        + [pl.BlockSpec(memory_space=pl.ANY) for _ in waits]
    )
    out_shape = [shape if c else jax.ShapeDtypeStruct((1, rows, width), jnp.float32) for c in coded]
    for m in moves:
        like = sources[m[0][0]]
        out_shape.append(jax.ShapeDtypeStruct((sum(n for _, _, n in m), like.shape[1]), like.dtype))
    n_copies = count * (blocks + 1) + sum(len(m) + 1 for m in moves) + blocks
    scratch = [
        pltpu.VMEM((blocks, count * tokens, block), acts.dtype),
        pltpu.VMEM((count * tokens, width), grads.dtype),
        pltpu.VMEM((groups, rows, width), jnp.float32),
        pltpu.VMEM((groups if any(coded) else 1, *(shape.shape if any(coded) else (TAIL, LANES))), jnp.int16),
        pltpu.SemaphoreType.DMA((n_copies,)),
    ] + [pltpu.VMEM(x.shape, x.dtype) for x in out_shape[groups:]]
    return pl.pallas_call(
        functools.partial(
            token_kernel,
            owners=owners,
            sizes=sizes,
            n_codes=len(codes),
            n_sources=len(sources),
            n_waits=len(waits),
            coded=coded,
            moves=moves,
            rows=rows,
            block=block,
        ),
        out_shape=out_shape,
        grid_spec=pltpu.PrefetchScalarGridSpec(
            num_scalar_prefetch=3,
            grid=(1,),
            in_specs=in_specs,
            out_specs=[pl.BlockSpec(memory_space=pl.ANY) for _ in out_shape],
            scratch_shapes=scratch,
        ),
        compiler_params=params(limit),
    )(where, slot, cycle, acts, grads, *codes, *sources, *waits)


def key_kernel(starts, current_ref, *refs, segments):
    out_ref, done_ref = refs[len(refs) - len(segments) - 3 : len(refs) - len(segments) - 1]
    blocks, sem = refs[len(refs) - len(segments) - 1 : -1], refs[-1]
    copies = []
    for n, (skip, rows) in enumerate(segments):
        step = min(rows, 512)
        for at in range(0, rows, step):
            size = min(step, rows - at)
            blocks[n][:, at : at + size] = lax.dot_general(
                current_ref[...],
                refs[n][skip + at : skip + at + size, :],
                (((1,), (1,)), ((), ())),
                preferred_element_type=jnp.float32,
            ).astype(out_ref.dtype)
        place = pl.ds(pl.multiple_of(starts[n], LANES), rows)
        copies.append(pltpu.make_async_copy(blocks[n], out_ref.at[:, place], sem.at[n]))
        copies[-1].start()
    done_ref[...] = jnp.zeros_like(done_ref)
    for c in copies:
        c.wait()


def key_products(current, parts, features, held, *waits):
    tokens, width = current.shape
    arrays = [x for x, _, _, _ in parts]
    anywhere = pl.BlockSpec(memory_space=pltpu.HBM)
    in_specs = [pl.BlockSpec(x.shape, lambda i, p: (0, 0)) for x in (current, *arrays)]
    operands = [jnp.stack([start for _, _, _, start in parts]), current, *arrays]
    aliases = {}
    if held is not None:
        in_specs.append(anywhere)
        aliases = {len(operands): 0}
        operands.append(held)
    in_specs += [pl.BlockSpec(memory_space=pl.ANY) for _ in waits]
    operands += waits
    return pl.pallas_call(
        functools.partial(key_kernel, segments=[(skip, rows) for _, skip, rows, _ in parts]),
        out_shape=[jax.ShapeDtypeStruct((tokens, features), jnp.bfloat16), DONE],
        grid_spec=pltpu.PrefetchScalarGridSpec(
            num_scalar_prefetch=1,
            grid=(1,),
            in_specs=in_specs,
            out_specs=[anywhere, pl.BlockSpec(DONE.shape, lambda i, p: (0, 0))],
            scratch_shapes=[pltpu.VMEM((tokens, rows), jnp.bfloat16) for _, _, rows, _ in parts]
            + [pltpu.SemaphoreType.DMA((len(parts),))],
        ),
        input_output_aliases=aliases,
        compiler_params=params(),
    )(*operands)


def decode_kernel(place, *refs, count, rows, width):
    out_ref, done_ref, code_refs, block_ref, sem = refs[-5:]
    slabs = width // LANES
    step = min(rows, 128)
    part = rows // CHUNKS
    copies = []

    def copy(source, target):
        copies.append(pltpu.make_async_copy(source, target, sem.at[len(copies)]))
        copies[-1].start()
        return copies[-1]

    coming = []
    for n in range(count):
        tail = pl.ds(slabs * rows, TAIL)
        coming.append([copy(refs[n].at[tail, :], code_refs.at[n, tail, :])])
        for k in range(CHUNKS):
            at = pl.ds(k * part * slabs, part * slabs)
            coming[n].append(copy(refs[n].at[at, :], code_refs.at[n, at, :]))
    leaving = []
    for n in range(count):
        coming[n][0].wait()
        scale = scale_of(code_refs.at[n], slabs * rows)

        def one(i, carry):
            r = pl.multiple_of(i * step, step)
            for j in range(slabs):
                block_ref[n, pl.ds(r, step), j * LANES : (j + 1) * LANES] = decoded(
                    code_refs.at[n], pl.multiple_of(r * slabs + j * step, step), step, scale
                )
            return carry

        for k in range(CHUNKS):
            coming[n][1 + k].wait()
            lax.fori_loop(k * part // step, (k + 1) * part // step, one, 0)
            at = pl.ds(k * part, part)
            leaving.append(copy(block_ref.at[n, at, :], out_ref.at[place[n], at, :]))
    done_ref[...] = jnp.zeros_like(done_ref)
    for c in leaving:
        c.wait()


def decode(place, codes, blocks, rows, width, held, *waits):
    count = len(codes)
    anywhere = pl.BlockSpec(memory_space=pltpu.HBM)
    in_specs = [pl.BlockSpec(memory_space=pl.ANY) for _ in codes]
    operands = [place, *codes]
    aliases = {}
    if held is not None:
        in_specs.append(anywhere)
        aliases = {len(operands): 0}
        operands.append(held)
    in_specs += [pl.BlockSpec(memory_space=pl.ANY) for _ in waits]
    operands += waits
    return pl.pallas_call(
        functools.partial(decode_kernel, count=count, rows=rows, width=width),
        out_shape=[jax.ShapeDtypeStruct((blocks, rows, width), jnp.float32), DONE],
        grid_spec=pltpu.PrefetchScalarGridSpec(
            num_scalar_prefetch=1,
            grid=(1,),
            in_specs=in_specs,
            out_specs=[anywhere, pl.BlockSpec(DONE.shape, lambda i, p: (0, 0))],
            scratch_shapes=[
                pltpu.VMEM((count, *codes[0].shape), jnp.int16),
                pltpu.VMEM((count, rows, width), jnp.float32),
                pltpu.SemaphoreType.DMA(((2 * CHUNKS + 1) * count,)),
            ],
        ),
        input_output_aliases=aliases,
        compiler_params=params(),
    )(*operands)


def body(acts, key_grads, weights, b_slot, cycle):
    stored, grads, weight = acts[0, 0], key_grads[0, 0], weights[0]
    micro, tokens, features = stored.shape
    width = grads.shape[2]
    n_dp, n_ctx = lax.axis_size("dp"), lax.axis_size("ctx")
    n_pipe = lax.axis_size("pipe")
    outer = n_dp // INNER
    replica, section = lax.axis_index("dp"), lax.axis_index("ctx")
    me_o, me_i = replica // INNER, replica % INNER
    groups = n_dp * n_ctx
    rows = features // groups
    pieces = cycle.shape[0]

    def swap(value):
        pairs = [(d, d // INNER * INNER + (d + 1) % INNER) for d in range(n_dp)]
        return lax.ppermute(value, "dp", pairs)

    def to_outer(value, by):
        return lax.ppermute(value, "dp", [(d, (d + by * INNER) % n_dp) for d in range(n_dp)])

    def to_ctx(value, by):
        return lax.ppermute(value, "ctx", [(d, (d + by) % n_ctx) for d in range(n_ctx)])

    def to_previous(value):
        return lax.ppermute(value, "pipe", [(d, d - 1) for d in range(1, n_pipe)])

    half = weight.shape[0] // INNER
    late_part = half // 2 // LANES * LANES

    block = min(rows, features // pieces, 512)
    far = [(kx, ko) for ko in range(1, outer) for kx in range(1, n_ctx)]
    near = [(0, ko) for ko in range(1, outer)]
    side = [(kx, 0) for kx in range(1, n_ctx)]
    home = [(0, 0)]
    where = jnp.stack([section, me_o, me_i]).astype(jnp.int32)
    sizes = (n_ctx, outer, features // pieces)

    def sent_by(wanted):
        return [(kx, ko, 1) for kx, ko in wanted]

    def kept_by(wanted):
        return [(kx, ko, 0) for kx, ko in wanted]

    def products(owners, coded, codes, *waits, limit=TOKEN_VMEM_LIMIT, **more):
        flags = coded if isinstance(coded, list) else [coded] * len(owners)
        return token_products(
            where, b_slot, cycle, sizes, owners, flags, stored, grads, block, rows, codes, *waits, limit=limit, **more
        )

    *far_out, own_all, own_most = products(
        sent_by(far) + kept_by(far),
        [True] * len(far) + [False] * len(far),
        [],
        sources=(weight, grads.reshape(micro * tokens, width)),
        moves=(
            [(0, lambda w, b: w[2] * half, half), (1, lambda w, b: b[0] * tokens, tokens)],
            [(0, lambda w, b: w[2] * half + late_part - PAD, half - late_part + PAD)],
        ),
        limit=FIRST_VMEM_LIMIT,
    )
    z_all = to_previous(own_all)
    crossed_most = [to_ctx(own_most, kx) for kx in range(1, n_ctx)]
    far_theirs = [swap(c) for c in far_out[: len(far)]]
    coded = {
        w: combine(kept, [theirs], tails=FAR_TAILS) for w, kept, theirs in zip(far, far_out[len(far) :], far_theirs)
    }
    got = {w: to_outer(coded[w], w[1]) for w in far}
    sent = products(sent_by(near + side), True, [], *coded.values())
    theirs = [swap(c) for c in sent]
    coded = dict(zip(near, products(kept_by(near), True, theirs[: len(near)], tails=SIDE_TAILS - 6)))
    side_sums = products(kept_by(side), False, theirs[len(near) :], *coded.values())

    passed = passed_done = None
    own_dones = []

    def pass_on(kx, start, pieces, *waits, apart=False):
        nonlocal passed, passed_done
        parts = []
        for piece, rows in pieces:
            row = ((section - kx) % n_ctx) * weight.shape[0] + start
            parts.append((piece, 0, rows, row + me_i * half))
            parts.append((swap(piece), 0, rows, row + (me_i + 1) % INNER * half))
            start = start + rows
        for some in (parts[0::2], parts[1::2]) if apart else (parts,):
            passed, passed_done = key_products(current, some, features, passed, *waits)
            own_dones.append(passed_done)
        return [x for x, _, _, _ in parts[1::2]]

    values = [
        combine(total, [got[kx, ko] for ko in range(1, outer)], tails=SIDE_TAILS + 1)
        for (kx, _), total in zip(side, side_sums)
    ]
    crossed = [to_ctx(v, kx) for (kx, _), v in zip(side, values)]
    got.update({w: to_outer(after(coded[w], *values), w[1]) for w in near})
    home_sent = products(sent_by(home), True, [], *values, *crossed_most)
    home_theirs = swap(home_sent[0])
    (home_kept,) = products(kept_by(home), False, [], home_sent[0])
    z_crossed = [to_previous(after(c, home_kept)) for c in crossed_most]
    z_first, z_second, late, current = split(
        z_all,
        (0, half // 2 + MORE),
        (half // 2, half - half // 2 + MORE),
        (0, late_part + LATE_PAD),
        (half, tokens),
    )
    z_pieces = [(z_first, half // 2), (z_second, half - half // 2)]
    codes = [home_theirs, *[got[0, ko] for ko in range(1, outer)], *crossed]
    own = combine(home_kept, codes, current, tails=4)
    others = {ko: to_outer(own, ko) for ko in range(1, outer)}
    late = [to_ctx(late, kx) for kx in range(1, n_ctx)]
    pass_on(0, 0, z_pieces)
    result, result_done = decode(
        jnp.stack([me_o * INNER + me_i, me_o * INNER + (me_i + 1) % INNER]),
        [own, swap(own)],
        n_dp,
        rows,
        width,
        None,
        passed_done,
    )
    most = half - late_part
    for kx in range(1, n_ctx):
        held = after(z_crossed[kx - 1], result_done)
        pass_on(kx, late_part, [(split(held, (PAD, most))[0], most)], apart=True)
    crossed_done = passed_done
    late = [after(x, own_dones[-2]) for x in late]
    late_theirs = []
    for kx in range(1, n_ctx):
        late_theirs += pass_on(kx, 0, [(split(late[kx - 1], (0, late_part))[0], late_part)])
    for ko in range(1, outer):
        other = after(others[ko], crossed_done, *late_theirs)
        o = (me_o - ko) % outer
        place = jnp.stack([o * INNER + me_i, o * INNER + (me_i + 1) % INNER])
        result, _ = decode(place, [other, swap(other)], n_dp, rows, width, result, passed_done)
    return passed[None, None], result.reshape(1, n_dp * rows, width)


def solution(mesh):
    placed = (
        P("dp", "pipe", None, "ctx", None),
        P("dp", "pipe", None, "ctx", None),
        P("pipe", "ctx", None),
        P("pipe"),
        P(),
    )
    return jax.shard_map(
        body,
        mesh=mesh,
        in_specs=placed,
        out_specs=(P("dp", "pipe", "ctx", None), P("pipe", "ctx", None)),
        check_vma=False,
    )
```

```python
import functools
import math

import jax
import jax.numpy as jnp
from jax import lax
from jax.experimental import pallas as pl
from jax.experimental.pallas import tpu as pltpu
from jax.sharding import PartitionSpec as P

LANES = 128
TAIL = 16
CHUNKS = 4
MORE = 32
PAD = 160
LATE_PAD = 48
FAR_TAILS = 3
SIDE_TAILS = 10
DONE = jax.ShapeDtypeStruct((8, LANES), jnp.float32)
INNER = 2
TOP = 32767.0
VMEM_LIMIT = 26 << 20
TOKEN_VMEM_LIMIT = 47 << 20
FIRST_VMEM_LIMIT = 47 << 20


def params(limit=VMEM_LIMIT):
    return pltpu.CompilerParams(vmem_limit_bytes=limit)


def code_shape(rows, width, tails=1):
    return jax.ShapeDtypeStruct((width // LANES * rows + TAIL * tails, LANES), jnp.int16)


def scale_of(code_ref, count):
    exponent = code_ref[count : count + TAIL, :].astype(jnp.int32)[0:1, :].astype(jnp.float32)
    return jnp.exp2(exponent) * (1.0 / (TOP * TOP))


def decoded(code_ref, start, rows, scale):
    level = code_ref[pl.ds(start, rows), :].astype(jnp.int32).astype(jnp.float32)
    return level * jnp.abs(level) * scale


def hold_kernel(*refs):
    pass


def after(value, *waits):
    return pl.pallas_call(
        hold_kernel,
        out_shape=jax.ShapeDtypeStruct(value.shape, value.dtype),
        in_specs=[pl.BlockSpec(memory_space=pl.ANY)] + [pl.BlockSpec(memory_space=pl.ANY) for _ in waits],
        out_specs=pl.BlockSpec(memory_space=pl.ANY),
        input_output_aliases={0: 0},
        compiler_params=params(),
    )(value, *waits)


def split_kernel(value_ref, *refs, cuts):
    outs, buffers, sem = refs[: len(cuts)], refs[len(cuts) : -1], refs[-1]
    coming = [
        pltpu.make_async_copy(value_ref.at[pl.ds(at, rows), :], buffers[n], sem.at[n])
        for n, (at, rows) in enumerate(cuts)
    ]
    leaving = [
        pltpu.make_async_copy(buffers[n], outs[n], sem.at[len(cuts) + n]) for n in range(len(cuts))
    ]
    for c in coming:
        c.start()
    for c, d in zip(coming, leaving):
        c.wait()
        d.start()
    for d in leaving:
        d.wait()


def split(value, *cuts):
    shapes = [jax.ShapeDtypeStruct((rows, value.shape[1]), value.dtype) for _, rows in cuts]
    return pl.pallas_call(
        functools.partial(split_kernel, cuts=cuts),
        out_shape=shapes,
        in_specs=[pl.BlockSpec(memory_space=pl.ANY)],
        out_specs=[pl.BlockSpec(memory_space=pl.ANY)] * len(cuts),
        scratch_shapes=[pltpu.VMEM(x.shape, x.dtype) for x in shapes]
        + [pltpu.SemaphoreType.DMA((2 * len(cuts),))],
        compiler_params=params(),
    )(value)


def gather_total(total_ref, start, rows, whole, codes, largest):
    width = total_ref.shape[1]
    step = min(rows, 128)
    slabs = width // LANES
    scales = [scale_of(c, slabs * whole) for c in codes]

    def add(i, largest):
        r = pl.multiple_of(start + i * step, step)
        for j in range(slabs):
            slab = slice(j * LANES, (j + 1) * LANES)
            value = total_ref[pl.ds(r, step), slab]
            for c, scale in zip(codes, scales):
                value = value + decoded(c, pl.multiple_of(r * slabs + j * step, step), step, scale)
            if codes:
                total_ref[pl.ds(r, step), slab] = value
            largest = jnp.maximum(largest, jnp.max(jnp.abs(value).reshape(step // 8, 8, LANES), axis=0))
        return largest

    return lax.fori_loop(0, rows // step, add, largest)


def encode(total_ref, largest, out_ref):
    rows, width = total_ref.shape
    step = min(rows, 128)
    slabs = width // LANES
    largest = jnp.max(jnp.max(largest, axis=0, keepdims=True), axis=1, keepdims=True)
    exponent = jnp.floor(jnp.log2(jnp.maximum(largest, 1e-30))) + 2.0
    exponent = jnp.broadcast_to(exponent, (8, LANES))
    shrink = jnp.exp2(-exponent)[0:1, :]

    def one(i, carry):
        r = pl.multiple_of(i * step, step)
        for j in range(slabs):
            value = total_ref[pl.ds(r, step), j * LANES : (j + 1) * LANES]
            root = jnp.round(jnp.sqrt(jnp.abs(value) * shrink) * TOP)
            level = jnp.where(value < 0.0, -root, root)
            place = pl.ds(pl.multiple_of(r * slabs + j * step, step), step)
            out_ref[place, :] = level.astype(jnp.int32).astype(jnp.int16)
        return carry

    lax.fori_loop(0, rows // step, one, 0)
    tail = jnp.concatenate([exponent] * ((out_ref.shape[0] - slabs * rows) // 8), axis=0)
    out_ref[slabs * rows :, :] = tail.astype(jnp.int32).astype(jnp.int16)


def combine_kernel(kept_ref, *refs, n_codes, rows):
    out_ref, total_ref = refs[-2:]
    total_ref[...] = kept_ref[0]
    largest = gather_total(total_ref, 0, rows, rows, refs[:n_codes], jnp.zeros((8, LANES), jnp.float32))
    encode(total_ref, largest, out_ref)


def combine(kept, codes, *waits, tails=1):
    _, rows, width = kept.shape
    shape = code_shape(rows, width, tails)
    in_specs = (
        [pl.BlockSpec((1, rows, width), lambda i: (0, 0, 0))]
        + [pl.BlockSpec(x.shape, lambda i: (0, 0)) for x in codes]
        + [pl.BlockSpec(memory_space=pl.ANY) for _ in waits]
    )
    return pl.pallas_call(
        functools.partial(combine_kernel, n_codes=len(codes), rows=rows),
        out_shape=shape,
        grid=(1,),
        in_specs=in_specs,
        out_specs=pl.BlockSpec(shape.shape, lambda i: (0, 0)),
        scratch_shapes=[pltpu.VMEM((rows, width), jnp.float32)],
        compiler_params=params(),
    )(kept, *codes, *waits)


def token_kernel(
    where,
    slot,
    cycle,
    acts_ref,
    grads_ref,
    *refs,
    owners,
    sizes,
    n_codes,
    n_sources,
    n_waits,
    coded,
    moves,
    rows,
    block,
):
    codes, sources, refs = refs[:n_codes], refs[n_codes : n_codes + n_sources], refs[n_codes + n_sources + n_waits :]
    groups = len(owners)
    outs, moved, refs = refs[:groups], refs[groups : groups + len(moves)], refs[groups + len(moves) :]
    left_ref, right_ref, total_refs, code_refs, sem = refs[:5]
    moving_refs = refs[5:]
    count, tokens = acts_ref.shape[0] - 1, grads_ref.shape[1]
    steps = rows // block
    n_ctx, outer, piece = sizes
    copies = []

    def copy(source, target):
        copies.append(pltpu.make_async_copy(source, target, sem.at[len(copies)]))
        copies[-1].start()
        return copies[-1]

    def pick(m):
        return m + (m >= slot[0]).astype(jnp.int32)

    def first_column(k):
        kx, ko, ki = owners[k // steps]
        ctx = lax.rem(where[0] + kx, n_ctx)
        replica = lax.rem(where[1] + ko, outer) * INNER + lax.rem(where[2] + ki, INNER)
        at = (ctx * (outer * INNER) + replica) * rows + k % steps * block
        return pl.multiple_of(cycle[at // piece] * piece + lax.rem(at, piece), block)

    ready = []
    for k in range(groups * steps):
        ready.append([])
        columns = pl.ds(first_column(k), block)
        for m in range(count):
            place = pl.ds(m * tokens, tokens)
            if k == 0:
                ready[0].append(copy(grads_ref.at[pick(m)], right_ref.at[place, :]))
            ready[k].append(copy(acts_ref.at[pick(m), :, columns], left_ref.at[k, place, :]))
    moving = []
    for buffer_ref, segments in zip(moving_refs, moves):
        place = 0
        for source, start, length in segments:
            there = pl.ds(pl.multiple_of(start(where, slot), TAIL), length)
            moving.append(copy(sources[source].at[there, :], buffer_ref.at[pl.ds(place, length), :]))
            place += length

    each = n_codes // groups
    leaving = []
    for n in range(groups):
        total_ref = total_refs.at[n]
        largest = jnp.zeros((8, LANES), jnp.float32)
        for b in range(steps):
            k = n * steps + b
            for c in ready[k]:
                c.wait()
            part = pl.ds(b * block, block)
            total_ref[part, :] = lax.dot_general(
                left_ref[k], right_ref[...], (((0,), (0,)), ((), ())), preferred_element_type=jnp.float32
            )
            if coded[n] or codes:
                largest = gather_total(total_ref, b * block, block, rows, codes[n * each : (n + 1) * each], largest)
            if not coded[n]:
                leaving.append(copy(total_ref.at[part, :], outs[n].at[0, part, :]))
        if coded[n]:
            encode(total_ref, largest, code_refs.at[n])
            leaving.append(copy(code_refs.at[n], outs[n]))
        if n == 0:
            for c in moving:
                c.wait()
            leaving += [copy(buffer_ref, out_ref) for buffer_ref, out_ref in zip(moving_refs, moved)]
    for c in leaving:
        c.wait()


def token_products(
    where, slot, cycle, sizes, owners, coded, acts, grads, block, rows, codes, *waits, tails=1, sources=(), moves=(), limit
):
    count = acts.shape[0] - 1
    tokens = acts.shape[1]
    width = grads.shape[2]
    groups = len(owners)
    blocks = groups * (rows // block)
    shape = code_shape(rows, width, tails)

    stays = pl.BlockSpec(memory_space=pltpu.HBM)
    in_specs = (
        [stays, stays]
        + [pl.BlockSpec(x.shape, lambda i, *_: (0, 0)) for x in codes]
        + [stays for _ in sources]
        + [pl.BlockSpec(memory_space=pl.ANY) for _ in waits]
    )
    out_shape = [shape if c else jax.ShapeDtypeStruct((1, rows, width), jnp.float32) for c in coded]
    for m in moves:
        like = sources[m[0][0]]
        out_shape.append(jax.ShapeDtypeStruct((sum(n for _, _, n in m), like.shape[1]), like.dtype))
    n_copies = count * (blocks + 1) + sum(len(m) + 1 for m in moves) + blocks
    scratch = [
        pltpu.VMEM((blocks, count * tokens, block), acts.dtype),
        pltpu.VMEM((count * tokens, width), grads.dtype),
        pltpu.VMEM((groups, rows, width), jnp.float32),
        pltpu.VMEM((groups if any(coded) else 1, *(shape.shape if any(coded) else (TAIL, LANES))), jnp.int16),
        pltpu.SemaphoreType.DMA((n_copies,)),
    ] + [pltpu.VMEM(x.shape, x.dtype) for x in out_shape[groups:]]
    return pl.pallas_call(
        functools.partial(
            token_kernel,
            owners=owners,
            sizes=sizes,
            n_codes=len(codes),
            n_sources=len(sources),
            n_waits=len(waits),
            coded=coded,
            moves=moves,
            rows=rows,
            block=block,
        ),
        out_shape=out_shape,
        grid_spec=pltpu.PrefetchScalarGridSpec(
            num_scalar_prefetch=3,
            grid=(1,),
            in_specs=in_specs,
            out_specs=[pl.BlockSpec(memory_space=pl.ANY) for _ in out_shape],
            scratch_shapes=scratch,
        ),
        compiler_params=params(limit),
    )(where, slot, cycle, acts, grads, *codes, *sources, *waits)


def key_kernel(starts, current_ref, *refs, segments):
    out_ref, done_ref = refs[len(refs) - len(segments) - 3 : len(refs) - len(segments) - 1]
    blocks, sem = refs[len(refs) - len(segments) - 1 : -1], refs[-1]
    copies = []
    for n, (skip, rows) in enumerate(segments):
        step = min(rows, 512)
        for at in range(0, rows, step):
            size = min(step, rows - at)
            blocks[n][:, at : at + size] = lax.dot_general(
                current_ref[...],
                refs[n][skip + at : skip + at + size, :],
                (((1,), (1,)), ((), ())),
                preferred_element_type=jnp.float32,
            ).astype(out_ref.dtype)
        place = pl.ds(pl.multiple_of(starts[n], LANES), rows)
        copies.append(pltpu.make_async_copy(blocks[n], out_ref.at[:, place], sem.at[n]))
        copies[-1].start()
    done_ref[...] = jnp.zeros_like(done_ref)
    for c in copies:
        c.wait()


def key_products(current, parts, features, held, *waits):
    tokens, width = current.shape
    arrays = [x for x, _, _, _ in parts]
    anywhere = pl.BlockSpec(memory_space=pltpu.HBM)
    in_specs = [pl.BlockSpec(x.shape, lambda i, p: (0, 0)) for x in (current, *arrays)]
    operands = [jnp.stack([start for _, _, _, start in parts]), current, *arrays]
    aliases = {}
    if held is not None:
        in_specs.append(anywhere)
        aliases = {len(operands): 0}
        operands.append(held)
    in_specs += [pl.BlockSpec(memory_space=pl.ANY) for _ in waits]
    operands += waits
    return pl.pallas_call(
        functools.partial(key_kernel, segments=[(skip, rows) for _, skip, rows, _ in parts]),
        out_shape=[jax.ShapeDtypeStruct((tokens, features), jnp.bfloat16), DONE],
        grid_spec=pltpu.PrefetchScalarGridSpec(
            num_scalar_prefetch=1,
            grid=(1,),
            in_specs=in_specs,
            out_specs=[anywhere, pl.BlockSpec(DONE.shape, lambda i, p: (0, 0))],
            scratch_shapes=[pltpu.VMEM((tokens, rows), jnp.bfloat16) for _, _, rows, _ in parts]
            + [pltpu.SemaphoreType.DMA((len(parts),))],
        ),
        input_output_aliases=aliases,
        compiler_params=params(),
    )(*operands)


def decode_kernel(place, *refs, count, rows, width):
    out_ref, done_ref, code_refs, block_ref, sem = refs[-5:]
    slabs = width // LANES
    step = min(rows, 128)
    part = rows // CHUNKS
    copies = []

    def copy(source, target):
        copies.append(pltpu.make_async_copy(source, target, sem.at[len(copies)]))
        copies[-1].start()
        return copies[-1]

    coming = []
    for n in range(count):
        tail = pl.ds(slabs * rows, TAIL)
        coming.append([copy(refs[n].at[tail, :], code_refs.at[n, tail, :])])
        for k in range(CHUNKS):
            at = pl.ds(k * part * slabs, part * slabs)
            coming[n].append(copy(refs[n].at[at, :], code_refs.at[n, at, :]))
    leaving = []
    for n in range(count):
        coming[n][0].wait()
        scale = scale_of(code_refs.at[n], slabs * rows)

        def one(i, carry):
            r = pl.multiple_of(i * step, step)
            for j in range(slabs):
                block_ref[n, pl.ds(r, step), j * LANES : (j + 1) * LANES] = decoded(
                    code_refs.at[n], pl.multiple_of(r * slabs + j * step, step), step, scale
                )
            return carry

        for k in range(CHUNKS):
            coming[n][1 + k].wait()
            lax.fori_loop(k * part // step, (k + 1) * part // step, one, 0)
            at = pl.ds(k * part, part)
            leaving.append(copy(block_ref.at[n, at, :], out_ref.at[place[n], at, :]))
    done_ref[...] = jnp.zeros_like(done_ref)
    for c in leaving:
        c.wait()


def decode(place, codes, blocks, rows, width, held, *waits):
    count = len(codes)
    anywhere = pl.BlockSpec(memory_space=pltpu.HBM)
    in_specs = [pl.BlockSpec(memory_space=pl.ANY) for _ in codes]
    operands = [place, *codes]
    aliases = {}
    if held is not None:
        in_specs.append(anywhere)
        aliases = {len(operands): 0}
        operands.append(held)
    in_specs += [pl.BlockSpec(memory_space=pl.ANY) for _ in waits]
    operands += waits
    return pl.pallas_call(
        functools.partial(decode_kernel, count=count, rows=rows, width=width),
        out_shape=[jax.ShapeDtypeStruct((blocks, rows, width), jnp.float32), DONE],
        grid_spec=pltpu.PrefetchScalarGridSpec(
            num_scalar_prefetch=1,
            grid=(1,),
            in_specs=in_specs,
            out_specs=[anywhere, pl.BlockSpec(DONE.shape, lambda i, p: (0, 0))],
            scratch_shapes=[
                pltpu.VMEM((count, *codes[0].shape), jnp.int16),
                pltpu.VMEM((count, rows, width), jnp.float32),
                pltpu.SemaphoreType.DMA(((2 * CHUNKS + 1) * count,)),
            ],
        ),
        input_output_aliases=aliases,
        compiler_params=params(),
    )(*operands)


def body(acts, key_grads, weights, b_slot, cycle):
    stored, grads, weight = acts[0, 0], key_grads[0, 0], weights[0]
    micro, tokens, features = stored.shape
    width = grads.shape[2]
    n_dp, n_ctx = lax.axis_size("dp"), lax.axis_size("ctx")
    n_pipe = lax.axis_size("pipe")
    outer = n_dp // INNER
    replica, section = lax.axis_index("dp"), lax.axis_index("ctx")
    me_o, me_i = replica // INNER, replica % INNER
    groups = n_dp * n_ctx
    rows = features // groups
    pieces = cycle.shape[0]

    def swap(value):
        pairs = [(d, d // INNER * INNER + (d + 1) % INNER) for d in range(n_dp)]
        return lax.ppermute(value, "dp", pairs)

    def to_outer(value, by):
        return lax.ppermute(value, "dp", [(d, (d + by * INNER) % n_dp) for d in range(n_dp)])

    def to_ctx(value, by):
        return lax.ppermute(value, "ctx", [(d, (d + by) % n_ctx) for d in range(n_ctx)])

    def to_previous(value):
        return lax.ppermute(value, "pipe", [(d, d - 1) for d in range(1, n_pipe)])

    half = weight.shape[0] // INNER
    late_part = half // 2 // LANES * LANES

    block = min(rows, features // pieces, 512)
    far = [(kx, ko) for ko in range(1, outer) for kx in range(1, n_ctx)]
    near = [(0, ko) for ko in range(1, outer)]
    side = [(kx, 0) for kx in range(1, n_ctx)]
    home = [(0, 0)]
    where = jnp.stack([section, me_o, me_i]).astype(jnp.int32)
    sizes = (n_ctx, outer, features // pieces)

    def sent_by(wanted):
        return [(kx, ko, 1) for kx, ko in wanted]

    def kept_by(wanted):
        return [(kx, ko, 0) for kx, ko in wanted]

    def products(owners, coded, codes, *waits, limit=TOKEN_VMEM_LIMIT, **more):
        flags = coded if isinstance(coded, list) else [coded] * len(owners)
        return token_products(
            where, b_slot, cycle, sizes, owners, flags, stored, grads, block, rows, codes, *waits, limit=limit, **more
        )

    *far_out, own_all, own_most = products(
        sent_by(far) + kept_by(far),
        [True] * len(far) + [False] * len(far),
        [],
        sources=(weight, grads.reshape(micro * tokens, width)),
        moves=(
            [(0, lambda w, b: w[2] * half, half), (1, lambda w, b: b[0] * tokens, tokens)],
            [(0, lambda w, b: w[2] * half + late_part - PAD, half - late_part + PAD)],
        ),
        limit=FIRST_VMEM_LIMIT,
    )
    z_all = to_previous(own_all)
    crossed_most = [to_ctx(own_most, kx) for kx in range(1, n_ctx)]
    far_theirs = [swap(c) for c in far_out[: len(far)]]
    coded = {
        w: combine(kept, [theirs], tails=FAR_TAILS) for w, kept, theirs in zip(far, far_out[len(far) :], far_theirs)
    }
    got = {w: to_outer(coded[w], w[1]) for w in far}
    sent = products(sent_by(near + side), True, [], *coded.values())
    theirs = [swap(c) for c in sent]
    coded = dict(zip(near, products(kept_by(near), True, theirs[: len(near)], tails=SIDE_TAILS - 6)))
    side_sums = products(kept_by(side), False, theirs[len(near) :], *coded.values())

    passed = passed_done = None
    own_dones = []

    def pass_on(kx, start, pieces, *waits, apart=False):
        nonlocal passed, passed_done
        parts = []
        for piece, rows in pieces:
            row = ((section - kx) % n_ctx) * weight.shape[0] + start
            parts.append((piece, 0, rows, row + me_i * half))
            parts.append((swap(piece), 0, rows, row + (me_i + 1) % INNER * half))
            start = start + rows
        for some in (parts[0::2], parts[1::2]) if apart else (parts,):
            passed, passed_done = key_products(current, some, features, passed, *waits)
            own_dones.append(passed_done)
        return [x for x, _, _, _ in parts[1::2]]

    values = [
        combine(total, [got[kx, ko] for ko in range(1, outer)], tails=SIDE_TAILS + 1)
        for (kx, _), total in zip(side, side_sums)
    ]
    crossed = [to_ctx(v, kx) for (kx, _), v in zip(side, values)]
    got.update({w: to_outer(after(coded[w], *values), w[1]) for w in near})
    home_sent = products(sent_by(home), True, [], *values, *crossed_most)
    home_theirs = swap(home_sent[0])
    (home_kept,) = products(kept_by(home), False, [], home_sent[0])
    z_crossed = [to_previous(after(c, home_kept)) for c in crossed_most]
    z_first, z_second, current = split(
        z_all, (0, late_part + LATE_PAD), (late_part, half - late_part + MORE), (half, tokens)
    )
    z_pieces = [(z_first, late_part), (z_second, half - late_part)]
    codes = [home_theirs, *[got[0, ko] for ko in range(1, outer)], *crossed]
    own = combine(home_kept, codes, current, tails=4)
    others = {ko: to_outer(own, ko) for ko in range(1, outer)}
    late = [to_ctx(z_first, kx) for kx in range(1, n_ctx)]
    pass_on(0, 0, z_pieces)
    result, result_done = decode(
        jnp.stack([me_o * INNER + me_i, me_o * INNER + (me_i + 1) % INNER]),
        [own, swap(own)],
        n_dp,
        rows,
        width,
        None,
        passed_done,
    )
    most = half - late_part
    for kx in range(1, n_ctx):
        held = after(z_crossed[kx - 1], result_done)
        pass_on(kx, late_part, [(split(held, (PAD, most))[0], most)], apart=True)
    crossed_done = passed_done
    late = [after(x, own_dones[-2]) for x in late]
    late_theirs = []
    for kx in range(1, n_ctx):
        late_theirs += pass_on(kx, 0, [(split(late[kx - 1], (0, late_part))[0], late_part)])
    for ko in range(1, outer):
        other = after(others[ko], crossed_done, *late_theirs)
        o = (me_o - ko) % outer
        place = jnp.stack([o * INNER + (me_i + 1) % INNER, o * INNER + me_i])
        result, _ = decode(place, [swap(other), other], n_dp, rows, width, result, passed_done)
    return passed[None, None], result.reshape(1, n_dp * rows, width)


def solution(mesh):
    placed = (
        P("dp", "pipe", None, "ctx", None),
        P("dp", "pipe", None, "ctx", None),
        P("pipe", "ctx", None),
        P("pipe"),
        P(),
    )
    return jax.shard_map(
        body,
        mesh=mesh,
        in_specs=placed,
        out_specs=(P("dp", "pipe", "ctx", None), P("pipe", "ctx", None)),
        check_vma=False,
    )
```

```python
import functools
import math

import jax
import jax.numpy as jnp
from jax import lax
from jax.experimental import pallas as pl
from jax.experimental.pallas import tpu as pltpu
from jax.sharding import PartitionSpec as P

LANES = 128
TAIL = 16
CHUNKS = 4
MORE = 32
PAD = 144
LATE_PAD = 48
FAR_TAILS = 3
SIDE_TAILS = 10
DONE = jax.ShapeDtypeStruct((8, LANES), jnp.float32)
INNER = 2
TOP = 32767.0
VMEM_LIMIT = 18 << 20
TOKEN_VMEM_LIMIT = 47 << 20
FIRST_VMEM_LIMIT = 47 << 20


def params(limit=VMEM_LIMIT):
    return pltpu.CompilerParams(vmem_limit_bytes=limit)


def code_shape(rows, width, tails=1):
    return jax.ShapeDtypeStruct((width // LANES * rows + TAIL * tails, LANES), jnp.int16)


def scale_of(code_ref, count):
    exponent = code_ref[count : count + TAIL, :].astype(jnp.int32)[0:1, :].astype(jnp.float32)
    return jnp.exp2(exponent) * (1.0 / (TOP * TOP))


def decoded(code_ref, start, rows, scale):
    level = code_ref[pl.ds(start, rows), :].astype(jnp.int32).astype(jnp.float32)
    return level * jnp.abs(level) * scale


def hold_kernel(*refs):
    pass


def after(value, *waits):
    return pl.pallas_call(
        hold_kernel,
        out_shape=jax.ShapeDtypeStruct(value.shape, value.dtype),
        in_specs=[pl.BlockSpec(memory_space=pl.ANY)] + [pl.BlockSpec(memory_space=pl.ANY) for _ in waits],
        out_specs=pl.BlockSpec(memory_space=pl.ANY),
        input_output_aliases={0: 0},
        compiler_params=params(),
    )(value, *waits)


def split_kernel(value_ref, *refs, cuts):
    outs, buffers, sem = refs[: len(cuts)], refs[len(cuts) : -1], refs[-1]
    coming = [
        pltpu.make_async_copy(value_ref.at[pl.ds(at, rows), :], buffers[n], sem.at[n])
        for n, (at, rows) in enumerate(cuts)
    ]
    leaving = [
        pltpu.make_async_copy(buffers[n], outs[n], sem.at[len(cuts) + n]) for n in range(len(cuts))
    ]
    for c in coming:
        c.start()
    for c, d in zip(coming, leaving):
        c.wait()
        d.start()
    for d in leaving:
        d.wait()


def split(value, *cuts):
    shapes = [jax.ShapeDtypeStruct((rows, value.shape[1]), value.dtype) for _, rows in cuts]
    return pl.pallas_call(
        functools.partial(split_kernel, cuts=cuts),
        out_shape=shapes,
        in_specs=[pl.BlockSpec(memory_space=pl.ANY)],
        out_specs=[pl.BlockSpec(memory_space=pl.ANY)] * len(cuts),
        scratch_shapes=[pltpu.VMEM(x.shape, x.dtype) for x in shapes]
        + [pltpu.SemaphoreType.DMA((2 * len(cuts),))],
        compiler_params=params(),
    )(value)


def gather_total(total_ref, start, rows, whole, codes, largest):
    width = total_ref.shape[1]
    step = min(rows, 128)
    slabs = width // LANES
    scales = [scale_of(c, slabs * whole) for c in codes]

    def add(i, largest):
        r = pl.multiple_of(start + i * step, step)
        for j in range(slabs):
            slab = slice(j * LANES, (j + 1) * LANES)
            value = total_ref[pl.ds(r, step), slab]
            for c, scale in zip(codes, scales):
                value = value + decoded(c, pl.multiple_of(r * slabs + j * step, step), step, scale)
            if codes:
                total_ref[pl.ds(r, step), slab] = value
            largest = jnp.maximum(largest, jnp.max(jnp.abs(value).reshape(step // 8, 8, LANES), axis=0))
        return largest

    return lax.fori_loop(0, rows // step, add, largest)


def encode(total_ref, largest, out_ref):
    rows, width = total_ref.shape
    step = min(rows, 128)
    slabs = width // LANES
    largest = jnp.max(jnp.max(largest, axis=0, keepdims=True), axis=1, keepdims=True)
    exponent = jnp.floor(jnp.log2(jnp.maximum(largest, 1e-30))) + 2.0
    exponent = jnp.broadcast_to(exponent, (8, LANES))
    shrink = jnp.exp2(-exponent)[0:1, :]

    def one(i, carry):
        r = pl.multiple_of(i * step, step)
        for j in range(slabs):
            value = total_ref[pl.ds(r, step), j * LANES : (j + 1) * LANES]
            root = jnp.round(jnp.sqrt(jnp.abs(value) * shrink) * TOP)
            level = jnp.where(value < 0.0, -root, root)
            place = pl.ds(pl.multiple_of(r * slabs + j * step, step), step)
            out_ref[place, :] = level.astype(jnp.int32).astype(jnp.int16)
        return carry

    lax.fori_loop(0, rows // step, one, 0)
    tail = jnp.concatenate([exponent] * ((out_ref.shape[0] - slabs * rows) // 8), axis=0)
    out_ref[slabs * rows :, :] = tail.astype(jnp.int32).astype(jnp.int16)


def combine_kernel(kept_ref, *refs, n_codes, rows):
    out_ref, total_ref = refs[-2:]
    total_ref[...] = kept_ref[0]
    largest = gather_total(total_ref, 0, rows, rows, refs[:n_codes], jnp.zeros((8, LANES), jnp.float32))
    encode(total_ref, largest, out_ref)


def combine(kept, codes, *waits, tails=1):
    _, rows, width = kept.shape
    shape = code_shape(rows, width, tails)
    in_specs = (
        [pl.BlockSpec((1, rows, width), lambda i: (0, 0, 0))]
        + [pl.BlockSpec(x.shape, lambda i: (0, 0)) for x in codes]
        + [pl.BlockSpec(memory_space=pl.ANY) for _ in waits]
    )
    return pl.pallas_call(
        functools.partial(combine_kernel, n_codes=len(codes), rows=rows),
        out_shape=shape,
        grid=(1,),
        in_specs=in_specs,
        out_specs=pl.BlockSpec(shape.shape, lambda i: (0, 0)),
        scratch_shapes=[pltpu.VMEM((rows, width), jnp.float32)],
        compiler_params=params(),
    )(kept, *codes, *waits)


def token_kernel(
    where,
    slot,
    cycle,
    acts_ref,
    grads_ref,
    *refs,
    owners,
    sizes,
    n_codes,
    n_sources,
    n_waits,
    coded,
    moves,
    rows,
    block,
):
    codes, sources, refs = refs[:n_codes], refs[n_codes : n_codes + n_sources], refs[n_codes + n_sources + n_waits :]
    groups = len(owners)
    outs, moved, refs = refs[:groups], refs[groups : groups + len(moves)], refs[groups + len(moves) :]
    left_ref, right_ref, total_refs, code_refs, sem = refs[:5]
    moving_refs = refs[5:]
    count, tokens = acts_ref.shape[0] - 1, grads_ref.shape[1]
    steps = rows // block
    n_ctx, outer, piece = sizes
    copies = []

    def copy(source, target):
        copies.append(pltpu.make_async_copy(source, target, sem.at[len(copies)]))
        copies[-1].start()
        return copies[-1]

    def pick(m):
        return m + (m >= slot[0]).astype(jnp.int32)

    def first_column(k):
        kx, ko, ki = owners[k // steps]
        ctx = lax.rem(where[0] + kx, n_ctx)
        replica = lax.rem(where[1] + ko, outer) * INNER + lax.rem(where[2] + ki, INNER)
        at = (ctx * (outer * INNER) + replica) * rows + k % steps * block
        return pl.multiple_of(cycle[at // piece] * piece + lax.rem(at, piece), block)

    ready = []
    for k in range(groups * steps):
        ready.append([])
        columns = pl.ds(first_column(k), block)
        for m in range(count):
            place = pl.ds(m * tokens, tokens)
            if k == 0:
                ready[0].append(copy(grads_ref.at[pick(m)], right_ref.at[place, :]))
            ready[k].append(copy(acts_ref.at[pick(m), :, columns], left_ref.at[k, place, :]))
    moving = []
    for buffer_ref, segments in zip(moving_refs, moves):
        place = 0
        for source, start, length in segments:
            there = pl.ds(pl.multiple_of(start(where, slot), TAIL), length)
            moving.append(copy(sources[source].at[there, :], buffer_ref.at[pl.ds(place, length), :]))
            place += length

    each = n_codes // groups
    leaving = []
    for n in range(groups):
        total_ref = total_refs.at[n]
        largest = jnp.zeros((8, LANES), jnp.float32)
        for b in range(steps):
            k = n * steps + b
            for c in ready[k]:
                c.wait()
            part = pl.ds(b * block, block)
            total_ref[part, :] = lax.dot_general(
                left_ref[k], right_ref[...], (((0,), (0,)), ((), ())), preferred_element_type=jnp.float32
            )
            if coded[n] or codes:
                largest = gather_total(total_ref, b * block, block, rows, codes[n * each : (n + 1) * each], largest)
            if not coded[n]:
                leaving.append(copy(total_ref.at[part, :], outs[n].at[0, part, :]))
        if coded[n]:
            encode(total_ref, largest, code_refs.at[n])
            leaving.append(copy(code_refs.at[n], outs[n]))
        if n == 0:
            for c in moving:
                c.wait()
            leaving += [copy(buffer_ref, out_ref) for buffer_ref, out_ref in zip(moving_refs, moved)]
    for c in leaving:
        c.wait()


def token_products(
    where, slot, cycle, sizes, owners, coded, acts, grads, block, rows, codes, *waits, tails=1, sources=(), moves=(), limit
):
    count = acts.shape[0] - 1
    tokens = acts.shape[1]
    width = grads.shape[2]
    groups = len(owners)
    blocks = groups * (rows // block)
    shape = code_shape(rows, width, tails)

    stays = pl.BlockSpec(memory_space=pltpu.HBM)
    in_specs = (
        [stays, stays]
        + [pl.BlockSpec(x.shape, lambda i, *_: (0, 0)) for x in codes]
        + [stays for _ in sources]
        + [pl.BlockSpec(memory_space=pl.ANY) for _ in waits]
    )
    out_shape = [shape if c else jax.ShapeDtypeStruct((1, rows, width), jnp.float32) for c in coded]
    for m in moves:
        like = sources[m[0][0]]
        out_shape.append(jax.ShapeDtypeStruct((sum(n for _, _, n in m), like.shape[1]), like.dtype))
    n_copies = count * (blocks + 1) + sum(len(m) + 1 for m in moves) + blocks
    scratch = [
        pltpu.VMEM((blocks, count * tokens, block), acts.dtype),
        pltpu.VMEM((count * tokens, width), grads.dtype),
        pltpu.VMEM((groups, rows, width), jnp.float32),
        pltpu.VMEM((groups if any(coded) else 1, *(shape.shape if any(coded) else (TAIL, LANES))), jnp.int16),
        pltpu.SemaphoreType.DMA((n_copies,)),
    ] + [pltpu.VMEM(x.shape, x.dtype) for x in out_shape[groups:]]
    return pl.pallas_call(
        functools.partial(
            token_kernel,
            owners=owners,
            sizes=sizes,
            n_codes=len(codes),
            n_sources=len(sources),
            n_waits=len(waits),
            coded=coded,
            moves=moves,
            rows=rows,
            block=block,
        ),
        out_shape=out_shape,
        grid_spec=pltpu.PrefetchScalarGridSpec(
            num_scalar_prefetch=3,
            grid=(1,),
            in_specs=in_specs,
            out_specs=[pl.BlockSpec(memory_space=pl.ANY) for _ in out_shape],
            scratch_shapes=scratch,
        ),
        compiler_params=params(limit),
    )(where, slot, cycle, acts, grads, *codes, *sources, *waits)


def key_kernel(starts, current_ref, *refs, segments):
    out_ref, done_ref = refs[len(refs) - len(segments) - 3 : len(refs) - len(segments) - 1]
    blocks, sem = refs[len(refs) - len(segments) - 1 : -1], refs[-1]
    copies = []
    for n, (skip, rows) in enumerate(segments):
        step = min(rows, 512)
        for at in range(0, rows, step):
            size = min(step, rows - at)
            blocks[n][:, at : at + size] = lax.dot_general(
                current_ref[...],
                refs[n][skip + at : skip + at + size, :],
                (((1,), (1,)), ((), ())),
                preferred_element_type=jnp.float32,
            ).astype(out_ref.dtype)
        place = pl.ds(pl.multiple_of(starts[n], LANES), rows)
        copies.append(pltpu.make_async_copy(blocks[n], out_ref.at[:, place], sem.at[n]))
        copies[-1].start()
    done_ref[...] = jnp.zeros_like(done_ref)
    for c in copies:
        c.wait()


def key_products(current, parts, features, held, *waits):
    tokens, width = current.shape
    arrays = [x for x, _, _, _ in parts]
    anywhere = pl.BlockSpec(memory_space=pltpu.HBM)
    in_specs = [pl.BlockSpec(x.shape, lambda i, p: (0, 0)) for x in (current, *arrays)]
    operands = [jnp.stack([start for _, _, _, start in parts]), current, *arrays]
    aliases = {}
    if held is not None:
        in_specs.append(anywhere)
        aliases = {len(operands): 0}
        operands.append(held)
    in_specs += [pl.BlockSpec(memory_space=pl.ANY) for _ in waits]
    operands += waits
    return pl.pallas_call(
        functools.partial(key_kernel, segments=[(skip, rows) for _, skip, rows, _ in parts]),
        out_shape=[jax.ShapeDtypeStruct((tokens, features), jnp.bfloat16), DONE],
        grid_spec=pltpu.PrefetchScalarGridSpec(
            num_scalar_prefetch=1,
            grid=(1,),
            in_specs=in_specs,
            out_specs=[anywhere, pl.BlockSpec(DONE.shape, lambda i, p: (0, 0))],
            scratch_shapes=[pltpu.VMEM((tokens, rows), jnp.bfloat16) for _, _, rows, _ in parts]
            + [pltpu.SemaphoreType.DMA((len(parts),))],
        ),
        input_output_aliases=aliases,
        compiler_params=params(),
    )(*operands)


def decode_kernel(place, *refs, count, rows, width):
    out_ref, done_ref, code_refs, block_ref, sem = refs[-5:]
    slabs = width // LANES
    step = min(rows, 128)
    part = rows // CHUNKS
    copies = []

    def copy(source, target):
        copies.append(pltpu.make_async_copy(source, target, sem.at[len(copies)]))
        copies[-1].start()
        return copies[-1]

    coming = []
    for n in range(count):
        tail = pl.ds(slabs * rows, TAIL)
        coming.append([copy(refs[n].at[tail, :], code_refs.at[n, tail, :])])
        for k in range(CHUNKS):
            at = pl.ds(k * part * slabs, part * slabs)
            coming[n].append(copy(refs[n].at[at, :], code_refs.at[n, at, :]))
    leaving = []
    for n in range(count):
        coming[n][0].wait()
        scale = scale_of(code_refs.at[n], slabs * rows)

        def one(i, carry):
            r = pl.multiple_of(i * step, step)
            for j in range(slabs):
                block_ref[n, pl.ds(r, step), j * LANES : (j + 1) * LANES] = decoded(
                    code_refs.at[n], pl.multiple_of(r * slabs + j * step, step), step, scale
                )
            return carry

        for k in range(CHUNKS):
            coming[n][1 + k].wait()
            lax.fori_loop(k * part // step, (k + 1) * part // step, one, 0)
            at = pl.ds(k * part, part)
            leaving.append(copy(block_ref.at[n, at, :], out_ref.at[place[n], at, :]))
    done_ref[...] = jnp.zeros_like(done_ref)
    for c in leaving:
        c.wait()


def decode(place, codes, blocks, rows, width, held, *waits):
    count = len(codes)
    anywhere = pl.BlockSpec(memory_space=pltpu.HBM)
    in_specs = [pl.BlockSpec(memory_space=pl.ANY) for _ in codes]
    operands = [place, *codes]
    aliases = {}
    if held is not None:
        in_specs.append(anywhere)
        aliases = {len(operands): 0}
        operands.append(held)
    in_specs += [pl.BlockSpec(memory_space=pl.ANY) for _ in waits]
    operands += waits
    return pl.pallas_call(
        functools.partial(decode_kernel, count=count, rows=rows, width=width),
        out_shape=[jax.ShapeDtypeStruct((blocks, rows, width), jnp.float32), DONE],
        grid_spec=pltpu.PrefetchScalarGridSpec(
            num_scalar_prefetch=1,
            grid=(1,),
            in_specs=in_specs,
            out_specs=[anywhere, pl.BlockSpec(DONE.shape, lambda i, p: (0, 0))],
            scratch_shapes=[
                pltpu.VMEM((count, *codes[0].shape), jnp.int16),
                pltpu.VMEM((count, rows, width), jnp.float32),
                pltpu.SemaphoreType.DMA(((2 * CHUNKS + 1) * count,)),
            ],
        ),
        input_output_aliases=aliases,
        compiler_params=params(),
    )(*operands)


def body(acts, key_grads, weights, b_slot, cycle):
    stored, grads, weight = acts[0, 0], key_grads[0, 0], weights[0]
    micro, tokens, features = stored.shape
    width = grads.shape[2]
    n_dp, n_ctx = lax.axis_size("dp"), lax.axis_size("ctx")
    n_pipe = lax.axis_size("pipe")
    outer = n_dp // INNER
    replica, section = lax.axis_index("dp"), lax.axis_index("ctx")
    me_o, me_i = replica // INNER, replica % INNER
    groups = n_dp * n_ctx
    rows = features // groups
    pieces = cycle.shape[0]

    def swap(value):
        pairs = [(d, d // INNER * INNER + (d + 1) % INNER) for d in range(n_dp)]
        return lax.ppermute(value, "dp", pairs)

    def to_outer(value, by):
        return lax.ppermute(value, "dp", [(d, (d + by * INNER) % n_dp) for d in range(n_dp)])

    def to_ctx(value, by):
        return lax.ppermute(value, "ctx", [(d, (d + by) % n_ctx) for d in range(n_ctx)])

    def to_previous(value):
        return lax.ppermute(value, "pipe", [(d, d - 1) for d in range(1, n_pipe)])

    half = weight.shape[0] // INNER
    late_part = half // 2 // LANES * LANES

    block = min(rows, features // pieces, 512)
    far = [(kx, ko) for ko in range(1, outer) for kx in range(1, n_ctx)]
    near = [(0, ko) for ko in range(1, outer)]
    side = [(kx, 0) for kx in range(1, n_ctx)]
    home = [(0, 0)]
    where = jnp.stack([section, me_o, me_i]).astype(jnp.int32)
    sizes = (n_ctx, outer, features // pieces)

    def sent_by(wanted):
        return [(kx, ko, 1) for kx, ko in wanted]

    def kept_by(wanted):
        return [(kx, ko, 0) for kx, ko in wanted]

    def products(owners, coded, codes, *waits, limit=TOKEN_VMEM_LIMIT, **more):
        flags = coded if isinstance(coded, list) else [coded] * len(owners)
        return token_products(
            where, b_slot, cycle, sizes, owners, flags, stored, grads, block, rows, codes, *waits, limit=limit, **more
        )

    *far_out, own_all, own_most = products(
        sent_by(far) + kept_by(far),
        [True] * len(far) + [False] * len(far),
        [],
        sources=(weight, grads.reshape(micro * tokens, width)),
        moves=(
            [(0, lambda w, b: w[2] * half, half), (1, lambda w, b: b[0] * tokens, tokens)],
            [(0, lambda w, b: w[2] * half + late_part - PAD, half - late_part + PAD)],
        ),
        limit=FIRST_VMEM_LIMIT,
    )
    z_all = to_previous(own_all)
    crossed_most = [to_ctx(own_most, kx) for kx in range(1, n_ctx)]
    far_theirs = [swap(c) for c in far_out[: len(far)]]
    coded = {
        w: combine(kept, [theirs], tails=FAR_TAILS) for w, kept, theirs in zip(far, far_out[len(far) :], far_theirs)
    }
    got = {w: to_outer(coded[w], w[1]) for w in far}
    sent = products(sent_by(near + side), True, [], *coded.values())
    theirs = [swap(c) for c in sent]
    coded = dict(zip(near, products(kept_by(near), True, theirs[: len(near)], tails=SIDE_TAILS - 6)))
    side_sums = products(kept_by(side), False, theirs[len(near) :], *coded.values())

    passed = passed_done = None
    own_dones = []

    def pass_on(kx, start, pieces, *waits, apart=False):
        nonlocal passed, passed_done
        parts = []
        for piece, rows in pieces:
            row = ((section - kx) % n_ctx) * weight.shape[0] + start
            parts.append((piece, 0, rows, row + me_i * half))
            parts.append((swap(piece), 0, rows, row + (me_i + 1) % INNER * half))
            start = start + rows
        for some in (parts[0::2], parts[1::2]) if apart else (parts,):
            passed, passed_done = key_products(current, some, features, passed, *waits)
            own_dones.append(passed_done)
        return [x for x, _, _, _ in parts[1::2]]

    values = [
        combine(total, [got[kx, ko] for ko in range(1, outer)], tails=SIDE_TAILS + 1)
        for (kx, _), total in zip(side, side_sums)
    ]
    crossed = [to_ctx(v, kx) for (kx, _), v in zip(side, values)]
    got.update({w: to_outer(after(coded[w], *values), w[1]) for w in near})
    home_sent = products(sent_by(home), True, [], *values, *crossed_most)
    home_theirs = swap(home_sent[0])
    (home_kept,) = products(kept_by(home), False, [], home_sent[0])
    z_crossed = [to_previous(after(c, home_kept)) for c in crossed_most]
    z_first, z_second, current = split(
        z_all, (0, late_part + LATE_PAD), (late_part, half - late_part + MORE), (half, tokens)
    )
    z_pieces = [(z_first, late_part), (z_second, half - late_part)]
    codes = [home_theirs, *[got[0, ko] for ko in range(1, outer)], *crossed]
    own = combine(home_kept, codes, current, tails=3)
    others = {ko: to_outer(own, ko) for ko in range(1, outer)}
    late = [to_ctx(z_first, kx) for kx in range(1, n_ctx)]
    pass_on(0, 0, z_pieces)
    result, result_done = decode(
        jnp.stack([me_o * INNER + me_i, me_o * INNER + (me_i + 1) % INNER]),
        [own, swap(own)],
        n_dp,
        rows,
        width,
        None,
        passed_done,
    )
    most = half - late_part
    for kx in range(1, n_ctx):
        held = after(z_crossed[kx - 1], result_done)
        pass_on(kx, late_part, [(split(held, (PAD, most))[0], most)], apart=True)
    crossed_done = passed_done
    late = [after(x, own_dones[-2]) for x in late]
    late_theirs = []
    for kx in range(1, n_ctx):
        late_theirs += pass_on(kx, 0, [(split(late[kx - 1], (0, late_part))[0], late_part)])
    for ko in range(1, outer):
        other = after(others[ko], crossed_done, *late_theirs)
        o = (me_o - ko) % outer
        place = jnp.stack([o * INNER + (me_i + 1) % INNER, o * INNER + me_i])
        result, _ = decode(place, [swap(other), other], n_dp, rows, width, result, passed_done)
    return passed[None, None], result.reshape(1, n_dp * rows, width)


def solution(mesh):
    placed = (
        P("dp", "pipe", None, "ctx", None),
        P("dp", "pipe", None, "ctx", None),
        P("pipe", "ctx", None),
        P("pipe"),
        P(),
    )
    return jax.shard_map(
        body,
        mesh=mesh,
        in_specs=placed,
        out_specs=(P("dp", "pipe", "ctx", None), P("pipe", "ctx", None)),
        check_vma=False,
    )
```
